256 devices in a mesh: row: 8 (over y, core), col: 32 (over x, z).
Axes of the slice: x: 4, y: 4, z: 8, core: 2. Of those that a mesh axis runs over, the one named last changes fastest.
Arguments:
- covariance: float32 [16384, 16384], P('row', 'col'), may hold values from 0 to 17.5, as said below
- observations: float32 [16384], P('row'), may hold values from -6 to 6
Outputs:
- updated: float32 [16384, 16384], P('row', 'col')
- factor: float32 [16384, 256], P('row')
- whitened: float32 [16384], P('row')
The draws below stay inside these ranges and needn't reach their ends.
Inputs may be any that keep to these rules, and one draw needn't show every extreme that they name: covariance rearranged to global order is symmetric and positive definite with every eigenvalue at least 0.5.
All inputs are finite; a program needn't handle non-finite values.
Results may differ from the reference program's by a relative error of at most 0.00019.
Values sent between devices are 32-bit elements; how exact they have to be, the bound alone decides.
A program may use at most 128 MiB of HBM per device.

```python
import jax
import jax.numpy as jnp
from jax import lax

TILE = 128
TC = 4
ORDER = 16384
ROWS_DEV = 2048
COLS_DEV = 512
N_ROW = 8
N_COL = 32


def draw_covariance(key, part):
    key = jax.random.fold_in(key, 11)
    key_pts, key_scale, key_nug = jax.random.split(key, 3)
    points = jax.random.uniform(key_pts, (ORDER, 2), jnp.float32)
    scales = jnp.exp(jax.random.uniform(key_scale, (ORDER,), jnp.float32, jnp.log(0.5), jnp.log(2.0)))
    nugget = jax.random.uniform(key_nug, (ORDER,), jnp.float32, 0.5, 1.5)
    stored = jnp.arange(ORDER, dtype=jnp.int32)
    row_glob = (stored % ROWS_DEV // TILE * N_ROW + stored // ROWS_DEV) * TILE + stored % TILE
    col_glob = (stored % COLS_DEV // TILE * N_COL + stored // COLS_DEV) * TILE + stored % TILE
    row_pts = points[row_glob]
    col_pts = points[col_glob]
    delta_x = row_pts[:, 0][:, None] - col_pts[:, 0][None, :]
    delta_y = row_pts[:, 1][:, None] - col_pts[:, 1][None, :]
    dist = jnp.sqrt(delta_x * delta_x + delta_y * delta_y)
    kernel = scales[row_glob][:, None] * scales[col_glob][None, :] * jnp.exp(-dist / 0.25)
    return kernel + jnp.where(row_glob[:, None] == col_glob[None, :], nugget[row_glob][:, None], 0.0)


def block_levels(stream_key, extent, shards, smallest, top_value):
    gain = 1.0
    for position, shards_of in shards:
        heights = jax.random.uniform(jax.random.fold_in(jax.random.fold_in(stream_key, 6), position), (shards_of,), jnp.float32, smallest / len(shards), top_value / len(shards))
        gain = gain * jnp.repeat(jnp.exp(heights), extent[position] // shards_of).reshape((-1,) + (1,) * (len(extent) - 1 - position))
    return gain


def bell_draw(key, shape, spread, reach, cuts=(), kind=jnp.bfloat16):
    values = spread * jax.random.normal(key, shape, jnp.float32)
    if cuts:
        values = values * block_levels(key, shape, cuts, -0.22, 0.18)
    return jnp.clip(values, -reach, reach).astype(kind)


def setup_inputs(seed: int = 0) -> dict:
    arg_keys = jax.random.split(jax.random.key(seed), 3)
    covariance = draw_covariance(jax.random.fold_in(arg_keys[2], 71), 0)
    observations = bell_draw(arg_keys[1], (ORDER,), 1.0, 6.0, ((0, 8),), jnp.float32)
    return dict(covariance=covariance, observations=observations)


HIGH = lax.Precision.HIGHEST

def first_panel(rows, diag_one):
    tile = diag_one.shape[0]
    return jax.scipy.linalg.solve_triangular(diag_one, rows[:, :tile].T, lower=True).T

def second_panel(rows, first_col, below_one):
    tile = below_one.shape[0]
    return rows[:, tile:2 * tile] - jnp.dot(first_col.astype(jnp.float32), below_one.T.astype(jnp.float32), precision=HIGH, preferred_element_type=jnp.float32)

def leading_factor(block):
    tile = block.shape[1] // 2
    diag_one = jnp.linalg.cholesky(block[:tile, :tile])
    first_col = first_panel(block, diag_one).at[:tile].set(diag_one)
    below_one = first_col[tile:2 * tile]
    residue = second_panel(block, first_col, below_one)
    diag_two = jnp.linalg.cholesky(residue[tile:2 * tile])
    second_col = jax.scipy.linalg.solve_triangular(diag_two, residue.T, lower=True).T
    second_col = second_col.at[:tile].set(jnp.zeros((tile, tile), jnp.float32)).at[tile:2 * tile].set(diag_two)
    return (jnp.concatenate([first_col, second_col], 1), diag_one, below_one, diag_two)

def panel_rows(rows, diag_one, below_one, diag_two):
    first_col = first_panel(rows, diag_one)
    residue = second_panel(rows, first_col, below_one)
    second_col = jax.scipy.linalg.solve_triangular(diag_two, residue.T, lower=True).T
    return jnp.concatenate([first_col, second_col], 1)

def reference(covariance, observations):
    row_tiles = TC * N_COL // N_ROW
    glob = covariance.reshape(N_ROW, row_tiles, TILE, N_COL, TC, TILE).transpose(1, 0, 2, 4, 3, 5).reshape(ORDER, ORDER)
    obs = observations.reshape(N_ROW, row_tiles, TILE).transpose(1, 0, 2).reshape(ORDER)
    lead, diag_one, below_one, diag_two = leading_factor(glob[:2 * TILE, :2 * TILE])
    lower = panel_rows(glob[:, :2 * TILE], diag_one, below_one, diag_two).at[:2 * TILE].set(lead)
    solved = jax.scipy.linalg.solve_triangular(lead, obs[:2 * TILE], lower=True)
    white = obs - jnp.dot(lower.astype(jnp.float32), solved.astype(jnp.float32), precision=HIGH, preferred_element_type=jnp.float32)
    white = white.at[:2 * TILE].set(solved)
    result = glob - jnp.dot(lower.astype(jnp.float32), lower.T.astype(jnp.float32), precision=HIGH, preferred_element_type=jnp.float32)
    result = result.reshape(row_tiles, N_ROW, TILE, TC, N_COL, TILE).transpose(1, 0, 2, 4, 3, 5).reshape(ORDER, ORDER)
    factor = lower.reshape(row_tiles, N_ROW, TILE, 2 * TILE).transpose(1, 0, 2, 3).reshape(ORDER, 2 * TILE)
    white = white.reshape(row_tiles, N_ROW, TILE).transpose(1, 0, 2).reshape(ORDER)
    return (result, factor, white)
```

```python
import jax
import jax.numpy as jnp
from jax import lax
from jax.experimental import pallas as pl
from jax.experimental.pallas import tpu as pltpu
from jax.sharding import PartitionSpec as P

MESH = pl.DeviceIdType.MESH
TILE = 128
PANEL = 2 * TILE
NB = 16
N_ROW, N_COL, NX, NZ = 8, 32, 4, 8
CHUNK = 64
ALPHA = 16
SLICE = TILE // NZ
F32, BF16 = jnp.float32, jnp.bfloat16


def split3(x):
    high = x.astype(BF16)
    rest = x - high.astype(F32)
    mid = rest.astype(BF16)
    return high, mid, (rest - mid.astype(F32)).astype(BF16)


def split2(x):
    high = x.astype(BF16)
    return high, (x - high.astype(F32)).astype(BF16)


def mul(a, b, dims):
    return lax.dot_general(a, b, (dims, ((), ())), preferred_element_type=F32)


def mul6(a, b, dims):
    ah, am, al = split3(a)
    bh, bm, bl = split3(b)
    small = mul(ah, bl, dims) + mul(al, bh, dims) + mul(am, bm, dims)
    return small + (mul(ah, bm, dims) + mul(am, bh, dims)) + mul(ah, bh, dims)


NN, NT, TN = ((1,), (0,)), ((1,), (1,)), ((0,), (0,))


def triangle(x, keep_lower):
    r = lax.broadcasted_iota(jnp.int32, (TILE, TILE), 0)
    c = lax.broadcasted_iota(jnp.int32, (TILE, TILE), 1)
    return jnp.where(r >= c if keep_lower else r <= c, x, 0.0)


def init_work(work, block):
    r = lax.broadcasted_iota(jnp.int32, (TILE, TILE), 0)
    c = lax.broadcasted_iota(jnp.int32, (TILE, TILE), 1)
    work[:, :TILE] = block
    work[:, TILE:] = jnp.where(r == c, 1.0, 0.0).astype(F32)


def eliminate(g, work):
    base = g * NB
    here = pl.ds(pl.multiple_of(base, NB), NB)
    rows = work[here, :]
    turned = pltpu.roll(rows[:, :TILE], lax.rem(TILE - base, TILE), 1)
    cols = [jnp.broadcast_to(turned[:, j : j + 1], (NB, TILE)) for j in range(NB)]
    el = [[jnp.broadcast_to(cols[j][i : i + 1, :], (8, TILE)) for j in range(i + 1)] for i in range(NB)]
    left = [jnp.broadcast_to(rows[i : i + 1, :TILE], (8, TILE)) for i in range(NB)]
    right = [jnp.broadcast_to(rows[i : i + 1, TILE:], (8, TILE)) for i in range(NB)]
    for j in range(NB):
        inv = lax.rsqrt(el[j][j])
        left[j] = left[j] * inv
        right[j] = right[j] * inv
        low = [None] * NB
        for i in range(j + 1, NB):
            low[i] = el[i][j] * inv
        for i in range(j + 1, NB):
            for k in range(j + 1, i + 1):
                el[i][k] = el[i][k] - low[i] * low[k]
            left[i] = left[i] - low[i] * left[j]
            right[i] = right[i] - low[i] * right[j]
    sub = lax.broadcasted_iota(jnp.int32, (8, TILE), 0)

    def pack(parts):
        halves = []
        for h in range(NB // 8):
            acc = parts[h * 8]
            for i in range(1, 8):
                acc = jnp.where(sub == i, parts[h * 8 + i], acc)
            halves.append(acc)
        return jnp.concatenate(halves, 0)

    u_left, u_right = pack(left), pack(right)
    lane = lax.broadcasted_iota(jnp.int32, (NB, TILE), 1)
    below = jnp.where(lane >= base + NB, u_left, 0.0)
    u = jnp.concatenate([u_left, u_right], 1)
    h, m, l = split3(u)
    hb, mb, lb = split3(below)
    lhs = jnp.concatenate([hb, hb, mb, mb, hb, lb], 0)
    rhs = jnp.concatenate([h, m, h, m, l, h], 0)
    work[...] = work[...] - mul(lhs, rhs, TN)
    work[here, :] = u


def gather_kernel(
    cov, obs, pan, cols, heads, lead_out, inv_out,
    lead, turn, work, saved,
    load_sem, l1_send, l1_recv, l2_send, l2_recv, l3_send, l3_recv, sib_send, sib_recv,
    sc_send, sc_recv, z_send, z_recv, x_send, x_recv, a_send, a_recv, b_send, b_recv,
    c_send, c_recv, h_send, h_recv,
):
    r, c = lax.axis_index("row"), lax.axis_index("col")
    y, k = r // 2, r % 2
    x, z = c // NZ, c % NZ
    sib = r + 1 - 2 * k

    def dev(rr, cc):
        return {"row": rr, "col": cc}

    def x_peer(i):
        return ((x + i) % NX) * NZ + z

    def z_peer(i):
        return x * NZ + (z + i) % NZ

    def remote(src, dst, send, recv, rr, cc):
        return pltpu.make_async_remote_copy(
            src_ref=src, dst_ref=dst, send_sem=send, recv_sem=recv, device_id=dev(rr, cc), device_id_type=MESH
        )

    at_source = r < 2
    in_root_plane = c < NZ

    @pl.when(at_source)
    def _():
        pltpu.make_async_copy(cov.at[0:TILE, :], saved, load_sem.at[0]).start()

    barrier = pltpu.get_barrier_semaphore()

    def hello(rr, cc):
        pl.semaphore_signal(barrier, inc=1, device_id=dev(rr, cc), device_id_type=MESH)

    for i in range(1, NX):
        hello(r, x_peer(i))
    for i in range(1, NZ):
        hello(r, z_peer(i))
    for i in range(1, 4):
        hello((r + 2 * i) % N_ROW, c)
    hello(sib, c)
    hello(0, x * NZ + r)
    hello(1, x * NZ + r)
    hello(k, z)
    due = 14 + jnp.where(at_source, NZ, 0) + jnp.where(at_source & in_root_plane, 16, 0)
    pl.semaphore_wait(barrier, due)

    def level_one(block, owner):
        for i in range(NZ):
            rows = slice(SLICE * i, SLICE * (i + 1))

            @pl.when(z != i)
            def _():
                remote(
                    cov.at[rows, 0:TILE], lead.at[i, block], l1_send.at[i], l1_recv.at[block], r, i
                ).start()

            @pl.when(z == i)
            def _():
                pltpu.make_async_copy(cov.at[rows, 0:TILE], lead.at[i, block], l1_recv.at[block]).start()

    @pl.when((r == 0) & (c == 0))
    def _():
        level_one(0, 0)

    @pl.when((r == 1) & (c == 0))
    def _():
        level_one(1, 0)

    @pl.when((r == 1) & (c == 1))
    def _():
        level_one(2, 1)

    def wait_bytes(ref, sem):
        pltpu.make_async_copy(ref, ref, sem).wait()

    def mine(kk):
        return lead.at[z, 0:1] if kk == 0 else lead.at[z, 1:3]

    for kk in range(2):

        @pl.when((r == kk) & in_root_plane)
        def _():
            if kk == 0:
                wait_bytes(lead.at[z, 0], l1_recv.at[0])
            else:
                wait_bytes(lead.at[z, 1], l1_recv.at[1])
                wait_bytes(lead.at[z, 2], l1_recv.at[2])
            for yy in range(4):
                for xx in range(NX):
                    if (yy, xx) != (0, 0):
                        remote(
                            mine(kk), mine(kk), l2_send.at[yy * NX + xx], l2_recv, 2 * yy + kk, xx * NZ + z
                        ).start()

    is_root_line = at_source & in_root_plane
    for kk in range(2):

        @pl.when(k == kk)
        def _():
            @pl.when(jnp.logical_not(is_root_line))
            def _():
                wait_bytes(mine(kk), l2_recv)

            for i in range(1, NZ):
                remote(mine(kk), mine(kk), l3_send.at[i], l3_recv.at[z], r, z_peer(i)).start()

    @pl.when(at_source)
    def _():
        pltpu.make_async_copy(cov.at[0:TILE, :], saved, load_sem.at[0]).wait()
        for s in range(4):
            turn[s] = saved[:, s * TILE : (s + 1) * TILE].T
        for kk in range(2):

            @pl.when(r == kk)
            def _():
                for i in range(NZ):
                    src = turn.at[i // 2, CHUNK * (i % 2) : CHUNK * (i % 2 + 1), :]
                    dst = pan.at[i // 2, x, i % 2, :, kk * TILE : (kk + 1) * TILE]

                    @pl.when((z == kk) & (z == i))
                    def _():
                        pltpu.make_async_copy(src, dst, sc_recv.at[kk]).start()

                    @pl.when(jnp.logical_not((z == kk) & (z == i)))
                    def _():
                        remote(src, dst, sc_send.at[i], sc_recv.at[kk], z, x * NZ + i).start()

    for kk in range(2):

        @pl.when(r == kk)
        def _():
            pltpu.make_async_copy(cov.at[0:TILE, :], cols.at[kk], c_recv.at[0]).start()
            pltpu.make_async_copy(obs.at[0:8, :], heads.at[kk], h_recv.at[0]).start()
            for i in range(1, 4):
                rr = (r + 2 * i) % N_ROW
                remote(cov.at[0:TILE, :], cols.at[kk], c_send.at[i], c_recv.at[0], rr, c).start()
                remote(obs.at[0:8, :], heads.at[kk], h_send.at[i], h_recv.at[0], rr, c).start()

    def gathered(kk, zz):
        return lead.at[zz, 0:1] if kk == 0 else lead.at[zz, 1:3]

    def whole(kk):
        return lead.at[:, 0:1] if kk == 0 else lead.at[:, 1:3]

    for kk in range(2):

        @pl.when(k == kk)
        def _():
            for i in range(1, NZ):
                zz = (z + i) % NZ
                wait_bytes(gathered(kk, zz), l3_recv.at[zz])
            remote(whole(kk), whole(kk), sib_send, sib_recv, sib, c).start()

    own = pan.at[z // 2, x, z % 2]
    for kk in range(2):
        wait_bytes(pan.at[z // 2, x, z % 2, :, kk * TILE : (kk + 1) * TILE], sc_recv.at[kk])
    for i in range(1, NX):
        remote(own, own, x_send.at[i], x_recv.at[x], r, x_peer(i)).start()
    for i in range(1, NZ):
        remote(own, own, z_send.at[i], z_recv.at[z], r, z_peer(i)).start()

    def forward_x(i):
        xx = (x + i) % NX
        wait_bytes(pan.at[z // 2, xx, z % 2], x_recv.at[xx])
        part = pan.at[z // 2, xx, z % 2, 0:ALPHA, :]
        for j in range(1, NZ):
            remote(part, part, a_send.at[i, j], a_recv.at[xx, z], r, z_peer(j)).start()

    def forward_z(i):
        zz = (z + i) % NZ
        wait_bytes(pan.at[zz // 2, x, zz % 2], z_recv.at[zz])
        part = pan.at[zz // 2, x, zz % 2, ALPHA:CHUNK, :]
        for j in range(1, NX):
            remote(part, part, b_send.at[i, j], b_recv.at[x, zz], r, x_peer(j)).start()

    for kk in range(2):

        @pl.when(k != kk)
        def _():
            wait_bytes(whole(kk), sib_recv)

    def block(b):
        return lead[:, b].reshape(TILE, TILE)

    init_work(work, block(0))

    def first(g, _):
        eliminate(g, work)

        @pl.when((g >= 0) & (g < 3))
        def _():
            forward_x(g + 1)

        @pl.when((g >= 1) & (g < 8))
        def _():
            n = g - 1
            forward_z(jnp.where(n % 2 == 0, n // 2 + 1, NZ - 1 - n // 2))

        return 0

    lax.fori_loop(0, TILE // NB, first, 0)
    diag_t = triangle(work[:, :TILE], False)
    inv_one = triangle(work[:, TILE:], True)
    lead_out[0:TILE, 0:TILE] = diag_t.T
    lead_out[0:TILE, TILE:PANEL] = jnp.zeros((TILE, TILE), F32)
    inv_out[0:TILE, 0:TILE] = inv_one
    inv_out[0:TILE, TILE:PANEL] = jnp.zeros((TILE, TILE), F32)
    below = mul6(block(1), inv_one, NT)
    lead_out[TILE:PANEL, 0:TILE] = below
    init_work(work, block(2) - mul6(below, below, NT))
    joint = mul6(below, inv_one, NN)

    for kk in range(2):

        @pl.when(k == kk)
        def _():
            wait_bytes(cols.at[kk], c_recv.at[0])
            wait_bytes(heads.at[kk], h_recv.at[0])
            remote(cols.at[kk], cols.at[kk], c_send.at[0], c_recv.at[1], sib, c).start()
            remote(heads.at[kk], heads.at[kk], h_send.at[0], h_recv.at[1], sib, c).start()

    def second(g, _):
        eliminate(g, work)
        return 0

    lax.fori_loop(0, TILE // NB, second, 0)
    inv_two = triangle(work[:, TILE:], True)
    lead_out[TILE:PANEL, TILE:PANEL] = triangle(work[:, :TILE], False).T
    inv_out[TILE:PANEL, TILE:PANEL] = inv_two
    inv_out[TILE:PANEL, 0:TILE] = -mul6(inv_two, joint, NN)

    for kk in range(2):

        @pl.when(k != kk)
        def _():
            wait_bytes(cols.at[kk], c_recv.at[1])
            wait_bytes(heads.at[kk], h_recv.at[1])

    for i in range(1, NX):
        xx = (x + i) % NX
        for j in range(1, NZ):
            zz = (z + j) % NZ
            wait_bytes(pan.at[zz // 2, xx, zz % 2, 0:ALPHA, :], a_recv.at[xx, zz])
            wait_bytes(pan.at[zz // 2, xx, zz % 2, ALPHA:CHUNK, :], b_recv.at[xx, zz])

    for i in range(1, NX):
        wait_bytes(own, x_send.at[i])
        for j in range(1, NZ):
            wait_bytes(pan.at[z // 2, 0, z % 2, 0:ALPHA, :], a_send.at[i, j])
    for i in range(1, NZ):
        wait_bytes(own, z_send.at[i])
        for j in range(1, NX):
            wait_bytes(pan.at[0, x, 0, ALPHA:CHUNK, :], b_send.at[i, j])
    for kk in range(2):

        @pl.when(k == kk)
        def _():
            for i in range(1, NZ):
                wait_bytes(mine(kk), l3_send.at[i])
            wait_bytes(whole(kk), sib_send)
            wait_bytes(cols.at[kk], c_send.at[0])
            wait_bytes(heads.at[kk], h_send.at[0])

        @pl.when(r == kk)
        def _():
            for i in range(1, 4):
                wait_bytes(cols.at[kk], c_send.at[i])
                wait_bytes(heads.at[kk], h_send.at[i])
            for i in range(NZ):

                @pl.when(jnp.logical_not((z == kk) & (z == i)))
                def _():
                    wait_bytes(turn.at[0, 0:CHUNK, :], sc_send.at[i])

        @pl.when((r == kk) & in_root_plane)
        def _():
            for i in range(1, 16):
                wait_bytes(mine(kk), l2_send.at[i])

    @pl.when(((r < 2) & (c == 0)) | ((r == 1) & (c == 1)))
    def _():
        for i in range(NZ):

            @pl.when(z != i)
            def _():
                wait_bytes(lead.at[0, 0], l1_send.at[i])


def update_kernel(cov, pan, obs, cols, heads, lead, inv, out, fac, white, inv_t, col_h, col_l, z_rows):
    step = pl.program_id(0)
    r = lax.axis_index("row")
    n = fac.shape[0]

    @pl.when(step == 0)
    def _():
        h, m, l = split3(inv[...].T)
        inv_t[0], inv_t[1], inv_t[2] = h, m, l
        h, l = split2(mul6(inv[...], cols[...], NN))
        col_h[...], col_l[...] = h, l
        first = jnp.concatenate([heads[0, 0:1, :], heads[1, 0:1, :]], 1)
        z_rows[...] = mul6(jnp.broadcast_to(first, (8, PANEL)), inv[...], NT)

    p_h, p_m, p_l = split3(pan[...])
    small = mul(p_h, inv_t[2], NN) + mul(p_l, inv_t[0], NN) + mul(p_m, inv_t[1], NN)
    rows = small + (mul(p_h, inv_t[1], NN) + mul(p_m, inv_t[0], NN)) + mul(p_h, inv_t[0], NN)
    fac[...] = rows

    @pl.when((step == 0) & (r < 2))
    def _():
        fac[0:TILE, :] = lead[pl.ds(pl.multiple_of(jnp.minimum(r, 1) * TILE, TILE), TILE), :]

    rows = fac[...]
    f_h, f_l = split2(rows)
    out[...] = cov[...] - (mul(f_h, col_l[...], NN) + mul(f_l, col_h[...], NN) + mul(f_h, col_h[...], NN))
    shift = mul6(z_rows[...], rows, NT)[0:1, :]
    for j in range(n // TILE):
        at = pl.ds(step * (n // TILE) + j, 1)
        white[at, :] = obs[at, :] - shift[:, j * TILE : (j + 1) * TILE]

    @pl.when((step == 0) & (r == 0))
    def _():
        white[0:1, :] = z_rows[0:1, 0:TILE]

    @pl.when((step == 0) & (r == 1))
    def _():
        white[0:1, :] = z_rows[0:1, TILE:PANEL]


def per_device(covariance, observations):
    obs = observations.reshape(16, TILE)
    dma = pltpu.SemaphoreType.DMA
    hbm = pl.BlockSpec(memory_space=pl.ANY)
    vmem = pl.BlockSpec(memory_space=pltpu.VMEM)
    pan, cols, heads, lead, inv = pl.pallas_call(
        gather_kernel,
        out_shape=[
            jax.ShapeDtypeStruct((4, NX, 2, CHUNK, PANEL), F32),
            jax.ShapeDtypeStruct((2, TILE, 512), F32),
            jax.ShapeDtypeStruct((2, 8, TILE), F32),
            jax.ShapeDtypeStruct((PANEL, PANEL), F32),
            jax.ShapeDtypeStruct((PANEL, PANEL), F32),
        ],
        in_specs=[hbm, hbm],
        out_specs=[hbm, hbm, hbm, vmem, vmem],
        scratch_shapes=[
            pltpu.VMEM((NZ, 3, SLICE, TILE), F32),
            pltpu.VMEM((4, TILE, TILE), F32),
            pltpu.VMEM((TILE, PANEL), F32),
            pltpu.VMEM((TILE, 512), F32),
            dma((1,)),
            dma((8,)), dma((3,)), dma((16,)), dma, dma((8,)), dma((8,)), dma, dma,
            dma((8,)), dma((2,)), dma((8,)), dma((8,)), dma((4,)), dma((4,)),
            dma((4, 8)), dma((4, 8)), dma((8, 4)), dma((4, 8)),
            dma((4,)), dma((2,)), dma((4,)), dma((2,)),
        ],
        compiler_params=pltpu.CompilerParams(collective_id=0, has_side_effects=True, vmem_limit_bytes=32 << 20),
    )(covariance, obs)
    rows = 256
    fixed = lambda *shape: pl.BlockSpec(shape, lambda i: (0,) * len(shape))
    out, fac, white = pl.pallas_call(
        update_kernel,
        grid=(2048 // rows,),
        out_shape=[
            jax.ShapeDtypeStruct((2048, 512), F32),
            jax.ShapeDtypeStruct((2048, PANEL), F32),
            jax.ShapeDtypeStruct((16, TILE), F32),
        ],
        in_specs=[
            pl.BlockSpec((rows, 512), lambda i: (i, 0)),
            pl.BlockSpec((rows, PANEL), lambda i: (i, 0)),
            fixed(16, TILE),
            fixed(PANEL, 512),
            fixed(2, 8, TILE),
            fixed(PANEL, PANEL),
            fixed(PANEL, PANEL),
        ],
        out_specs=[
            pl.BlockSpec((rows, 512), lambda i: (i, 0)),
            pl.BlockSpec((rows, PANEL), lambda i: (i, 0)),
            fixed(16, TILE),
        ],
        scratch_shapes=[
            pltpu.VMEM((3, PANEL, PANEL), BF16),
            pltpu.VMEM((PANEL, 512), BF16),
            pltpu.VMEM((PANEL, 512), BF16),
            pltpu.VMEM((8, PANEL), F32),
        ],
        compiler_params=pltpu.CompilerParams(vmem_limit_bytes=32 << 20),
    )(covariance, pan.reshape(2048, PANEL), obs, cols.reshape(PANEL, 512), heads, lead, inv)
    return out, fac, white.reshape(2048)


def solution(mesh):
    placed = (P("row", "col"), P("row"))
    return jax.shard_map(
        per_device,
        mesh=mesh,
        in_specs=placed,
        out_specs=(P("row", "col"), P("row", None), P("row")),
        check_vma=False,
    )
```

```python
import jax
import jax.numpy as jnp
from jax import lax
from jax.experimental import pallas as pl
from jax.experimental.pallas import tpu as pltpu
from jax.sharding import PartitionSpec as P

MESH = pl.DeviceIdType.MESH
TILE = 128
PANEL = 2 * TILE
NB = 16
N_ROW, N_COL, NX, NZ = 8, 32, 4, 8
CHUNK = 64
HALF = CHUNK // 2
QUARTER = CHUNK // 4
PARTS = 4
SLICE = TILE // NZ
F32, BF16 = jnp.float32, jnp.bfloat16


def split3(x):
    high = x.astype(BF16)
    rest = x - high.astype(F32)
    mid = rest.astype(BF16)
    return high, mid, (rest - mid.astype(F32)).astype(BF16)


def split2(x):
    high = x.astype(BF16)
    return high, (x - high.astype(F32)).astype(BF16)


def mul(a, b, dims):
    return lax.dot_general(a, b, (dims, ((), ())), preferred_element_type=F32)


def mul6(a, b, dims):
    ah, am, al = split3(a)
    bh, bm, bl = split3(b)
    small = mul(ah, bl, dims) + mul(al, bh, dims) + mul(am, bm, dims)
    return small + (mul(ah, bm, dims) + mul(am, bh, dims)) + mul(ah, bh, dims)


NN, NT, TN = ((1,), (0,)), ((1,), (1,)), ((0,), (0,))


def triangle(x, keep_lower):
    r = lax.broadcasted_iota(jnp.int32, (TILE, TILE), 0)
    c = lax.broadcasted_iota(jnp.int32, (TILE, TILE), 1)
    return jnp.where(r >= c if keep_lower else r <= c, x, 0.0)


def init_work(work, block):
    r = lax.broadcasted_iota(jnp.int32, (TILE, TILE), 0)
    c = lax.broadcasted_iota(jnp.int32, (TILE, TILE), 1)
    work[:, :TILE] = block
    work[:, TILE:] = jnp.where(r == c, 1.0, 0.0).astype(F32)


def eliminate(g, work):
    base = g * NB
    here = pl.ds(pl.multiple_of(base, NB), NB)
    rows = work[here, :]
    turned = pltpu.roll(rows[:, :TILE], lax.rem(TILE - base, TILE), 1)
    cols = [jnp.broadcast_to(turned[:, j : j + 1], (NB, TILE)) for j in range(NB)]
    el = [[jnp.broadcast_to(cols[j][i : i + 1, :], (8, TILE)) for j in range(i + 1)] for i in range(NB)]
    left = [jnp.broadcast_to(rows[i : i + 1, :TILE], (8, TILE)) for i in range(NB)]
    right = [jnp.broadcast_to(rows[i : i + 1, TILE:], (8, TILE)) for i in range(NB)]
    for j in range(NB):
        inv = lax.rsqrt(el[j][j])
        left[j] = left[j] * inv
        right[j] = right[j] * inv
        low = [None] * NB
        for i in range(j + 1, NB):
            low[i] = el[i][j] * inv
        for i in range(j + 1, NB):
            for k in range(j + 1, i + 1):
                el[i][k] = el[i][k] - low[i] * low[k]
            left[i] = left[i] - low[i] * left[j]
            right[i] = right[i] - low[i] * right[j]
    sub = lax.broadcasted_iota(jnp.int32, (8, TILE), 0)

    def pack(parts):
        halves = []
        for h in range(NB // 8):
            acc = parts[h * 8]
            for i in range(1, 8):
                acc = jnp.where(sub == i, parts[h * 8 + i], acc)
            halves.append(acc)
        return jnp.concatenate(halves, 0)

    u_left, u_right = pack(left), pack(right)
    lane = lax.broadcasted_iota(jnp.int32, (NB, TILE), 1)
    below = jnp.where(lane >= base + NB, u_left, 0.0)
    u = jnp.concatenate([u_left, u_right], 1)
    h, m, l = split3(u)
    hb, mb, lb = split3(below)
    lhs = jnp.concatenate([hb, hb, mb, mb, hb, lb], 0)
    rhs = jnp.concatenate([h, m, h, m, l, h], 0)
    work[...] = work[...] - mul(lhs, rhs, TN)
    work[here, :] = u


def gather_kernel(
    cov, obs, pan, cols, heads, inv_out, cov_here, obs_here,
    lead, turn, work, saved,
    load_sem, l1_send, l1_recv, l2_send, l2_recv, l3_send, l3_recv, sib_send, sib_recv,
    sc_send, sc_recv, x_send, x_recv, up_send, up_recv, down_send, down_recv, side_send, side_recv,
    c_send, c_recv, h_send, h_recv,
):
    r, c = lax.axis_index("row"), lax.axis_index("col")
    y, k = r // 2, r % 2
    x, z = c // NZ, c % NZ
    sib = r + 1 - 2 * k

    def dev(rr, cc):
        return {"row": rr, "col": cc}

    def x_peer(i):
        return ((x + i) % NX) * NZ + z

    def z_peer(i):
        return x * NZ + (z + i) % NZ

    def remote(src, dst, send, recv, rr, cc):
        return pltpu.make_async_remote_copy(
            src_ref=src, dst_ref=dst, send_sem=send, recv_sem=recv, device_id=dev(rr, cc), device_id_type=MESH
        )

    at_source = r < 2
    in_root_plane = c < NZ

    @pl.when(at_source)
    def _():
        pltpu.make_async_copy(cov.at[0:TILE, :], saved, load_sem.at[0]).start()

    barrier = pltpu.get_barrier_semaphore()

    def hello(rr, cc):
        pl.semaphore_signal(barrier, inc=1, device_id=dev(rr, cc), device_id_type=MESH)

    for i in range(1, NX):
        hello(r, x_peer(i))
    for i in range(1, NZ):
        hello(r, z_peer(i))
    for i in range(1, 4):
        hello((r + 2 * i) % N_ROW, c)
    hello(sib, c)
    hello(0, x * NZ + r)
    hello(1, x * NZ + r)
    hello(k, z)
    @pl.when(at_source)
    def _():
        pltpu.make_async_copy(cov.at[0:TILE, :], saved, load_sem.at[0]).wait()
        for s in range(4):
            turn[s] = saved[:, s * TILE : (s + 1) * TILE].T

    due = 14 + jnp.where(at_source, NZ, 0) + jnp.where(at_source & in_root_plane, 16, 0)
    pl.semaphore_wait(barrier, due)

    def level_one(block, owner):
        for i in range(NZ):
            rows = slice(SLICE * i, SLICE * (i + 1))

            @pl.when(z != i)
            def _():
                remote(
                    cov.at[rows, 0:TILE], lead.at[i, block], l1_send.at[i], l1_recv.at[block], r, i
                ).start()

            @pl.when(z == i)
            def _():
                pltpu.make_async_copy(cov.at[rows, 0:TILE], lead.at[i, block], l1_recv.at[block]).start()

    @pl.when((r == 0) & (c == 0))
    def _():
        level_one(0, 0)

    @pl.when((r == 1) & (c == 0))
    def _():
        level_one(1, 0)

    @pl.when((r == 1) & (c == 1))
    def _():
        level_one(2, 1)

    def wait_bytes(ref, sem):
        pltpu.make_async_copy(ref, ref, sem).wait()

    def mine(kk):
        return lead.at[z, 0:1] if kk == 0 else lead.at[z, 1:3]

    for kk in range(2):

        @pl.when((r == kk) & in_root_plane)
        def _():
            if kk == 0:
                wait_bytes(lead.at[z, 0], l1_recv.at[0])
            else:
                wait_bytes(lead.at[z, 1], l1_recv.at[1])
                wait_bytes(lead.at[z, 2], l1_recv.at[2])
            for yy in range(4):
                for xx in range(NX):
                    if (yy, xx) != (0, 0):
                        remote(
                            mine(kk), mine(kk), l2_send.at[yy * NX + xx], l2_recv, 2 * yy + kk, xx * NZ + z
                        ).start()

    is_root_line = at_source & in_root_plane
    for kk in range(2):

        @pl.when(k == kk)
        def _():
            @pl.when(jnp.logical_not(is_root_line))
            def _():
                wait_bytes(mine(kk), l2_recv)

            for i in range(1, NZ):
                remote(mine(kk), mine(kk), l3_send.at[i], l3_recv.at[z], r, z_peer(i)).start()

    @pl.when(at_source)
    def _():
        for kk in range(2):

            @pl.when(r == kk)
            def _():
                for i in range(NZ):
                    src = turn.at[i // 2, CHUNK * (i % 2) : CHUNK * (i % 2 + 1), :]
                    dst = pan.at[i // 2, x, i % 2, :, kk * TILE : (kk + 1) * TILE]

                    @pl.when((z == kk) & (z == i))
                    def _():
                        pltpu.make_async_copy(src, dst, sc_recv.at[kk]).start()

                    @pl.when(jnp.logical_not((z == kk) & (z == i)))
                    def _():
                        remote(src, dst, sc_send.at[i], sc_recv.at[kk], z, x * NZ + i).start()

    own = pan.at[z // 2, x, z % 2]
    for kk in range(2):
        wait_bytes(pan.at[z // 2, x, z % 2, :, kk * TILE : (kk + 1) * TILE], sc_recv.at[kk])

    def chunk(xx, zz, first, count):
        return pan.at[zz // 2, xx, zz % 2, first : first + count, :]

    def pass_on(i, d, first, count):
        xx = (x + i) % NX
        for way, send, recv in ((1, up_send, up_recv), (-1, down_send, down_recv)):
            zz = (z - way * (d - 1) + NZ) % NZ
            low, rows = first, count
            if d == NZ // 2:
                rows = count // 2
                low = first if way == 1 else first + rows
            part = chunk(xx, zz, low, rows)
            remote(part, part, send.at[i, d], recv.at[i, d], r, x * NZ + (z + way + NZ) % NZ).start()

    def landed(i, d, first, count):
        xx = (x + i) % NX
        for way, recv in ((1, up_recv), (-1, down_recv)):
            zz = (z - way * d + NZ) % NZ
            low, rows = first, count
            if d == NZ // 2:
                rows = count // 2
                low = first if way == 1 else first + rows
            wait_bytes(chunk(xx, zz, low, rows), recv.at[i, d])

    def sideways(zz, d, way):
        part = chunk(x, zz, HALF, HALF)
        for j in range(1, NX):
            remote(part, part, side_send.at[d, j], side_recv.at[zz, x], r, x_peer(j)).start()

    def own_column(d):
        landed(0, d, 0, CHUNK)
        if d < NZ // 2:
            pass_on(0, d + 1, 0, CHUNK)
            sideways((z - d + NZ) % NZ, d, 1)
            sideways((z + d) % NZ, NZ - d, -1)
        else:
            sideways((z + d) % NZ, d, -1)

    def other_columns(d):
        for i in range(1, NX):
            landed(i, d, 0, HALF)
            if d < NZ // 2:
                pass_on(i, d + 1, 0, HALF)

    pass_on(0, 1, 0, CHUNK)
    for i in range(1, NX):
        remote(own, own, x_send.at[i], x_recv.at[x], r, x_peer(i)).start()

    for kk in range(2):

        @pl.when(r == kk)
        def _():
            pltpu.make_async_copy(cov.at[0:TILE, :], cols.at[kk], c_recv.at[0]).start()
            pltpu.make_async_copy(obs.at[0:8, :], heads.at[kk], h_recv.at[0]).start()
            for i in range(1, 4):
                rr = (r + 2 * i) % N_ROW
                remote(cov.at[0:TILE, :], cols.at[kk], c_send.at[i], c_recv.at[0], rr, c).start()
                remote(obs.at[0:8, :], heads.at[kk], h_send.at[i], h_recv.at[0], rr, c).start()

    load_cov = pltpu.make_async_copy(cov, cov_here, load_sem.at[1])
    load_cov.start()
    load_obs = pltpu.make_async_copy(obs, obs_here, load_sem.at[2])
    load_obs.start()

    own_column(1)
    for i in range(1, NX):
        xx = (x + i) % NX
        wait_bytes(chunk(xx, z, 0, CHUNK), x_recv.at[xx])
        pass_on(i, 1, 0, HALF)

    def gathered(kk, zz):
        return lead.at[zz, 0:1] if kk == 0 else lead.at[zz, 1:3]

    def whole(kk):
        return lead.at[:, 0:1] if kk == 0 else lead.at[:, 1:3]

    for kk in range(2):

        @pl.when(k == kk)
        def _():
            for i in range(1, NZ):
                zz = (z + i) % NZ
                wait_bytes(gathered(kk, zz), l3_recv.at[zz])
            remote(whole(kk), whole(kk), sib_send, sib_recv, sib, c).start()

    for kk in range(2):

        @pl.when(k != kk)
        def _():
            wait_bytes(whole(kk), sib_recv)

    def block(b):
        return lead[:, b].reshape(TILE, TILE)

    FIRST = (
        (1, lambda: own_column(2)),
        (2, lambda: other_columns(1)),
        (4, lambda: own_column(3)),
        (6, lambda: other_columns(2)),
    )
    SECOND = ((0, lambda: own_column(4)), (2, lambda: other_columns(3)))
    init_work(work, block(0))

    def first(g, _):
        eliminate(g, work)
        for at, service in FIRST:

            @pl.when(g == at)
            def _():
                service()

        return 0

    lax.fori_loop(0, TILE // NB, first, 0)
    inv_one = triangle(work[:, TILE:], True)
    inv_out[0:TILE, 0:TILE] = inv_one
    inv_out[0:TILE, TILE:PANEL] = jnp.zeros((TILE, TILE), F32)
    below = mul6(block(1), inv_one, NT)
    init_work(work, block(2) - mul6(below, below, NT))
    joint = mul6(below, inv_one, NN)

    for kk in range(2):

        @pl.when(k == kk)
        def _():
            wait_bytes(cols.at[kk], c_recv.at[0])
            wait_bytes(heads.at[kk], h_recv.at[0])
            remote(cols.at[kk], cols.at[kk], c_send.at[0], c_recv.at[1], sib, c).start()
            remote(heads.at[kk], heads.at[kk], h_send.at[0], h_recv.at[1], sib, c).start()

    def second(g, _):
        eliminate(g, work)
        for at, service in SECOND:

            @pl.when(g == at)
            def _():
                service()

        return 0

    lax.fori_loop(0, TILE // NB, second, 0)
    inv_two = triangle(work[:, TILE:], True)
    inv_out[TILE:PANEL, TILE:PANEL] = inv_two
    inv_out[TILE:PANEL, 0:TILE] = -mul6(inv_two, joint, NN)

    for kk in range(2):

        @pl.when(k != kk)
        def _():
            wait_bytes(cols.at[kk], c_recv.at[1])
            wait_bytes(heads.at[kk], h_recv.at[1])

    other_columns(NZ // 2)
    for i in range(1, NX):
        xx = (x + i) % NX
        for j in range(1, NZ):
            zz = (z + j) % NZ
            wait_bytes(chunk(xx, zz, HALF, HALF), side_recv.at[zz, xx])
    load_cov.wait()
    load_obs.wait()

    for i in range(NX):
        rows = CHUNK if i == 0 else HALF
        for d in range(1, NZ // 2 + 1):
            part = chunk(x, z, 0, rows if d < NZ // 2 else rows // 2)
            wait_bytes(part, up_send.at[i, d])
            wait_bytes(part, down_send.at[i, d])
    for j in range(1, NX):
        wait_bytes(own, x_send.at[j])
        for d in range(1, NZ):
            wait_bytes(chunk(x, z, HALF, HALF), side_send.at[d, j])
    for kk in range(2):

        @pl.when(k == kk)
        def _():
            for i in range(1, NZ):
                wait_bytes(mine(kk), l3_send.at[i])
            wait_bytes(whole(kk), sib_send)
            wait_bytes(cols.at[kk], c_send.at[0])
            wait_bytes(heads.at[kk], h_send.at[0])

        @pl.when(r == kk)
        def _():
            for i in range(1, 4):
                wait_bytes(cols.at[kk], c_send.at[i])
                wait_bytes(heads.at[kk], h_send.at[i])
            for i in range(NZ):

                @pl.when(jnp.logical_not((z == kk) & (z == i)))
                def _():
                    wait_bytes(turn.at[0, 0:CHUNK, :], sc_send.at[i])

        @pl.when((r == kk) & in_root_plane)
        def _():
            for i in range(1, 16):
                wait_bytes(mine(kk), l2_send.at[i])

    @pl.when(((r < 2) & (c == 0)) | ((r == 1) & (c == 1)))
    def _():
        for i in range(NZ):

            @pl.when(z != i)
            def _():
                wait_bytes(lead.at[0, 0], l1_send.at[i])


def update_kernel(cov, pan, obs, cols, heads, inv, out, fac, white, rows, done, sems):
    r = lax.axis_index("row")
    h, m, l = split3(inv[...].T)
    p_h, p_m, p_l = split3(pan[...])
    small = mul(p_h, l, NN) + mul(p_l, h, NN) + mul(p_m, m, NN)
    rows[...] = small + (mul(p_h, m, NN) + mul(p_m, h, NN)) + mul(p_h, h, NN)

    @pl.when(r == 0)
    def _():
        rows[0:TILE, 0:TILE] = triangle(rows[0:TILE, 0:TILE], True)
        rows[0:TILE, TILE:PANEL] = jnp.zeros((TILE, TILE), F32)

    @pl.when(r == 1)
    def _():
        rows[0:TILE, TILE:PANEL] = triangle(rows[0:TILE, TILE:PANEL], True)

    write_rows = pltpu.make_async_copy(rows, fac, sems.at[0])
    write_rows.start()
    c_h, c_l = split2(mul6(inv[...], cols[...], NN))
    first = jnp.concatenate([heads[0, 0:1, :], heads[1, 0:1, :]], 1)
    z_row = mul6(jnp.broadcast_to(first, (8, PANEL)), inv[...], NT)[0:1, :]
    writes = []
    for i in range(PARTS):
        n = 2048 // PARTS
        at = slice(i * n, (i + 1) * n)
        f_h, f_l = split2(rows[at, :])
        done[at, :] = cov[at, :] - (mul(f_h, c_l, NN) + mul(f_l, c_h, NN) + mul(f_h, c_h, NN))
        copy = pltpu.make_async_copy(done.at[at, :], out.at[at, :], sems.at[1 + i])
        copy.start()
        writes.append(copy)
    lane = lax.broadcasted_iota(jnp.int32, (TILE, TILE), 1)
    acc = jnp.zeros((TILE, TILE), F32)
    for t in range(16):
        part = jnp.sum(rows[t * TILE : (t + 1) * TILE, :] * z_row, axis=1, keepdims=True)
        acc = jnp.where(lane == t, part, acc)
    white[...] = obs[...] - acc.T[0:16]

    @pl.when(r == 0)
    def _():
        white[0:1, :] = z_row[:, 0:TILE]

    @pl.when(r == 1)
    def _():
        white[0:1, :] = z_row[:, TILE:PANEL]

    write_rows.wait()
    for copy in writes:
        copy.wait()


def per_device(covariance, observations):
    obs = observations.reshape(16, TILE)
    dma = pltpu.SemaphoreType.DMA
    any_space = pl.BlockSpec(memory_space=pl.ANY)
    hbm = pl.BlockSpec(memory_space=pltpu.HBM)
    vmem = pl.BlockSpec(memory_space=pltpu.VMEM)
    pan, cols, heads, inv, cov_here, obs_here = pl.pallas_call(
        gather_kernel,
        out_shape=[
            jax.ShapeDtypeStruct((4, NX, 2, CHUNK, PANEL), F32),
            jax.ShapeDtypeStruct((2, TILE, 512), F32),
            jax.ShapeDtypeStruct((2, 8, TILE), F32),
            jax.ShapeDtypeStruct((PANEL, PANEL), F32),
            jax.ShapeDtypeStruct((2048, 512), F32),
            jax.ShapeDtypeStruct((16, TILE), F32),
        ],
        in_specs=[hbm, hbm],
        out_specs=[any_space, any_space, any_space, vmem, any_space, any_space],
        scratch_shapes=[
            pltpu.VMEM((NZ, 3, SLICE, TILE), F32),
            pltpu.VMEM((4, TILE, TILE), F32),
            pltpu.VMEM((TILE, PANEL), F32),
            pltpu.VMEM((TILE, 512), F32),
            dma((3,)),
            dma((8,)), dma((3,)), dma((16,)), dma, dma((8,)), dma((8,)), dma, dma,
            dma((8,)), dma((2,)), dma((4,)), dma((4,)),
            dma((4, 5)), dma((4, 5)), dma((4, 5)), dma((4, 5)), dma((8, 4)), dma((8, 4)),
            dma((4,)), dma((2,)), dma((4,)), dma((2,)),
        ],
        compiler_params=pltpu.CompilerParams(collective_id=0, has_side_effects=True, vmem_limit_bytes=46 << 20),
    )(covariance, obs)
    out, fac, white = pl.pallas_call(
        update_kernel,
        out_shape=[
            jax.ShapeDtypeStruct((2048, 512), F32),
            jax.ShapeDtypeStruct((2048, PANEL), F32),
            jax.ShapeDtypeStruct((16, TILE), F32),
        ],
        in_specs=[vmem] * 6,
        out_specs=[any_space, any_space, vmem],
        scratch_shapes=[
            pltpu.VMEM((2048, PANEL), F32),
            pltpu.VMEM((2048, 512), F32),
            dma((1 + PARTS,)),
        ],
        compiler_params=pltpu.CompilerParams(vmem_limit_bytes=36 << 20),
    )(cov_here, pan.reshape(2048, PANEL), obs_here, cols.reshape(PANEL, 512), heads, inv)
    return out, fac, white.reshape(2048)


def solution(mesh):
    placed = (P("row", "col"), P("row"))
    return jax.shard_map(
        per_device,
        mesh=mesh,
        in_specs=placed,
        out_specs=(P("row", "col"), P("row", None), P("row")),
        check_vma=False,
    )
```

```python
import jax
import jax.numpy as jnp
from jax import lax
from jax.experimental import pallas as pl
from jax.experimental.pallas import tpu as pltpu
from jax.sharding import PartitionSpec as P

MESH = pl.DeviceIdType.MESH
TILE = 128
PANEL = 2 * TILE
NB = 16
N_ROW, N_COL, NX, NZ = 8, 32, 4, 8
CHUNK = 64
HALF = CHUNK // 2
QUARTER = CHUNK // 4
PARTS = 4
SLICE = TILE // NZ
F32, BF16 = jnp.float32, jnp.bfloat16


def split3(x):
    high = x.astype(BF16)
    rest = x - high.astype(F32)
    mid = rest.astype(BF16)
    return high, mid, (rest - mid.astype(F32)).astype(BF16)


def split2(x):
    high = x.astype(BF16)
    return high, (x - high.astype(F32)).astype(BF16)


def mul(a, b, dims):
    return lax.dot_general(a, b, (dims, ((), ())), preferred_element_type=F32)


def mul6(a, b, dims):
    ah, am, al = split3(a)
    bh, bm, bl = split3(b)
    small = mul(ah, bl, dims) + mul(al, bh, dims) + mul(am, bm, dims)
    return small + (mul(ah, bm, dims) + mul(am, bh, dims)) + mul(ah, bh, dims)


NN, NT, TN = ((1,), (0,)), ((1,), (1,)), ((0,), (0,))


def triangle(x, keep_lower):
    r = lax.broadcasted_iota(jnp.int32, (TILE, TILE), 0)
    c = lax.broadcasted_iota(jnp.int32, (TILE, TILE), 1)
    return jnp.where(r >= c if keep_lower else r <= c, x, 0.0)


def init_work(work, block):
    r = lax.broadcasted_iota(jnp.int32, (TILE, TILE), 0)
    c = lax.broadcasted_iota(jnp.int32, (TILE, TILE), 1)
    work[:, :TILE] = block
    work[:, TILE:] = jnp.where(r == c, 1.0, 0.0).astype(F32)


def eliminate(g, work):
    base = g * NB
    here = pl.ds(pl.multiple_of(base, NB), NB)
    rows = work[here, :]
    turned = pltpu.roll(rows[:, :TILE], lax.rem(TILE - base, TILE), 1)
    cols = [jnp.broadcast_to(turned[:, j : j + 1], (NB, TILE)) for j in range(NB)]
    el = [[jnp.broadcast_to(cols[j][i : i + 1, :], (8, TILE)) for j in range(i + 1)] for i in range(NB)]
    left = [jnp.broadcast_to(rows[i : i + 1, :TILE], (8, TILE)) for i in range(NB)]
    right = [jnp.broadcast_to(rows[i : i + 1, TILE:], (8, TILE)) for i in range(NB)]
    for j in range(NB):
        inv = lax.rsqrt(el[j][j])
        left[j] = left[j] * inv
        right[j] = right[j] * inv
        low = [None] * NB
        for i in range(j + 1, NB):
            low[i] = el[i][j] * inv
        for i in range(j + 1, NB):
            for k in range(j + 1, i + 1):
                el[i][k] = el[i][k] - low[i] * low[k]
            left[i] = left[i] - low[i] * left[j]
            right[i] = right[i] - low[i] * right[j]
    sub = lax.broadcasted_iota(jnp.int32, (8, TILE), 0)

    def pack(parts):
        halves = []
        for h in range(NB // 8):
            acc = parts[h * 8]
            for i in range(1, 8):
                acc = jnp.where(sub == i, parts[h * 8 + i], acc)
            halves.append(acc)
        return jnp.concatenate(halves, 0)

    u_left, u_right = pack(left), pack(right)
    lane = lax.broadcasted_iota(jnp.int32, (NB, TILE), 1)
    below = jnp.where(lane >= base + NB, u_left, 0.0)
    u = jnp.concatenate([u_left, u_right], 1)
    h, m, l = split3(u)
    hb, mb, lb = split3(below)
    lhs = jnp.concatenate([hb, hb, mb, mb, hb, lb], 0)
    rhs = jnp.concatenate([h, m, h, m, l, h], 0)
    work[...] = work[...] - mul(lhs, rhs, TN)
    work[here, :] = u


def gather_kernel(
    cov, obs, fac_here, cov_here, col_high, col_low, white,
    pan, cols, heads, obs_here, rows, inv, acc, lead, turn, work, saved,
    load_sem, out_sem, l1_send, l1_recv, l2_send, l2_recv, l3_send, l3_recv, sib_send, sib_recv,
    sc_send, sc_recv, x_send, x_recv, up_send, up_recv, down_send, down_recv, side_send, side_recv,
    c_send, c_recv, h_send, h_recv,
):
    r, c = lax.axis_index("row"), lax.axis_index("col")
    y, k = r // 2, r % 2
    x, z = c // NZ, c % NZ
    sib = r + 1 - 2 * k

    def dev(rr, cc):
        return {"row": rr, "col": cc}

    def x_peer(i):
        return ((x + i) % NX) * NZ + z

    def z_peer(i):
        return x * NZ + (z + i) % NZ

    def remote(src, dst, send, recv, rr, cc):
        return pltpu.make_async_remote_copy(
            src_ref=src, dst_ref=dst, send_sem=send, recv_sem=recv, device_id=dev(rr, cc), device_id_type=MESH
        )

    at_source = r < 2
    in_root_plane = c < NZ

    @pl.when(at_source)
    def _():
        pltpu.make_async_copy(cov.at[0:TILE, :], saved, load_sem.at[0]).start()

    barrier = pltpu.get_barrier_semaphore()

    def hello(rr, cc):
        pl.semaphore_signal(barrier, inc=1, device_id=dev(rr, cc), device_id_type=MESH)

    for i in range(1, NX):
        hello(r, x_peer(i))
    for i in range(1, NZ):
        hello(r, z_peer(i))
    for i in range(1, 4):
        hello((r + 2 * i) % N_ROW, c)
    hello(sib, c)
    hello(0, x * NZ + r)
    hello(1, x * NZ + r)
    hello(k, z)
    @pl.when(at_source)
    def _():
        pltpu.make_async_copy(cov.at[0:TILE, :], saved, load_sem.at[0]).wait()
        for s in range(4):
            turn[s] = saved[:, s * TILE : (s + 1) * TILE].T

    due = 14 + jnp.where(at_source, NZ, 0) + jnp.where(at_source & in_root_plane, 16, 0)
    pl.semaphore_wait(barrier, due)

    def level_one(block, owner):
        for i in range(NZ):
            rows = slice(SLICE * i, SLICE * (i + 1))

            @pl.when(z != i)
            def _():
                remote(
                    cov.at[rows, 0:TILE], lead.at[i, block], l1_send.at[i], l1_recv.at[block], r, i
                ).start()

            @pl.when(z == i)
            def _():
                pltpu.make_async_copy(cov.at[rows, 0:TILE], lead.at[i, block], l1_recv.at[block]).start()

    @pl.when((r == 0) & (c == 0))
    def _():
        level_one(0, 0)

    @pl.when((r == 1) & (c == 0))
    def _():
        level_one(1, 0)

    @pl.when((r == 1) & (c == 1))
    def _():
        level_one(2, 1)

    def wait_bytes(ref, sem):
        pltpu.make_async_copy(ref, ref, sem).wait()

    def mine(kk):
        return lead.at[z, 0:1] if kk == 0 else lead.at[z, 1:3]

    @pl.when(at_source)
    def _():
        for kk in range(2):

            @pl.when(r == kk)
            def _():
                for i in (4, 3, 5, 2, 6, 1, 7, 0):
                    zz = (z + i) % NZ
                    src = turn.at[zz // 2, pl.ds(pl.multiple_of(CHUNK * (zz % 2), CHUNK), CHUNK), :]
                    dst = pan.at[zz // 2, x, zz % 2, :, kk * TILE : (kk + 1) * TILE]
                    if i:
                        remote(src, dst, sc_send.at[i], sc_recv.at[kk], z, x * NZ + zz).start()
                    else:

                        @pl.when(z == kk)
                        def _():
                            pltpu.make_async_copy(src, dst, sc_recv.at[kk]).start()

                        @pl.when(z != kk)
                        def _():
                            remote(src, dst, sc_send.at[i], sc_recv.at[kk], z, x * NZ + zz).start()

    for kk in range(2):

        @pl.when((r == kk) & in_root_plane)
        def _():
            if kk == 0:
                wait_bytes(lead.at[z, 0], l1_recv.at[0])
            else:
                wait_bytes(lead.at[z, 1], l1_recv.at[1])
                wait_bytes(lead.at[z, 2], l1_recv.at[2])
            for yy in range(4):
                for xx in range(NX):
                    if (yy, xx) != (0, 0):
                        remote(
                            mine(kk), mine(kk), l2_send.at[yy * NX + xx], l2_recv, 2 * yy + kk, xx * NZ + z
                        ).start()

    is_root_line = at_source & in_root_plane
    for kk in range(2):

        @pl.when(k == kk)
        def _():
            @pl.when(jnp.logical_not(is_root_line))
            def _():
                wait_bytes(mine(kk), l2_recv)

            for i in range(1, NZ):
                remote(mine(kk), mine(kk), l3_send.at[i], l3_recv.at[z], r, z_peer(i)).start()

    own = pan.at[z // 2, x, z % 2]
    for kk in range(2):
        wait_bytes(pan.at[z // 2, x, z % 2, :, kk * TILE : (kk + 1) * TILE], sc_recv.at[kk])

    def chunk(xx, zz, first, count):
        return pan.at[zz // 2, xx, zz % 2, first : first + count, :]

    def pass_on(i, d, first, count):
        xx = (x + i) % NX
        for way, send, recv in ((1, up_send, up_recv), (-1, down_send, down_recv)):
            zz = (z - way * (d - 1) + NZ) % NZ
            low, rows = first, count
            if d == NZ // 2:
                rows = count // 2
                low = first if way == 1 else first + rows
            part = chunk(xx, zz, low, rows)
            remote(part, part, send.at[i, d], recv.at[i, d], r, x * NZ + (z + way + NZ) % NZ).start()

    def landed(i, d, first, count):
        xx = (x + i) % NX
        for way, recv in ((1, up_recv), (-1, down_recv)):
            zz = (z - way * d + NZ) % NZ
            low, rows = first, count
            if d == NZ // 2:
                rows = count // 2
                low = first if way == 1 else first + rows
            wait_bytes(chunk(xx, zz, low, rows), recv.at[i, d])

    def sideways(zz, d, way):
        part = chunk(x, zz, HALF, HALF)
        for j in range(1, NX):
            remote(part, part, side_send.at[d, j], side_recv.at[zz, x], r, x_peer(j)).start()

    def own_column(d):
        landed(0, d, 0, CHUNK)
        if d < NZ // 2:
            pass_on(0, d + 1, 0, CHUNK)
            sideways((z - d + NZ) % NZ, d, 1)
            sideways((z + d) % NZ, NZ - d, -1)
        else:
            sideways((z + d) % NZ, d, -1)

    def other_columns(d):
        for i in range(1, NX):
            landed(i, d, 0, HALF)
            if d < NZ // 2:
                pass_on(i, d + 1, 0, HALF)

    pass_on(0, 1, 0, CHUNK)
    for i in range(1, NX):
        remote(own, own, x_send.at[i], x_recv.at[x], r, x_peer(i)).start()

    for kk in range(2):

        @pl.when(r == kk)
        def _():
            pltpu.make_async_copy(cov.at[0:TILE, :], cols.at[kk], c_recv.at[0]).start()
            pltpu.make_async_copy(obs.at[0:8, :], heads.at[kk], h_recv.at[0]).start()
            for i in range(1, 4):
                rr = (r + 2 * i) % N_ROW
                remote(cov.at[0:TILE, :], cols.at[kk], c_send.at[i], c_recv.at[0], rr, c).start()
                remote(obs.at[0:8, :], heads.at[kk], h_send.at[i], h_recv.at[0], rr, c).start()

    load_cov = pltpu.make_async_copy(cov, cov_here, load_sem.at[1])
    load_cov.start()
    load_obs = pltpu.make_async_copy(obs, obs_here, load_sem.at[2])
    load_obs.start()

    own_column(1)
    for i in range(1, NX):
        xx = (x + i) % NX
        wait_bytes(chunk(xx, z, 0, CHUNK), x_recv.at[xx])
        pass_on(i, 1, 0, HALF)

    def gathered(kk, zz):
        return lead.at[zz, 0:1] if kk == 0 else lead.at[zz, 1:3]

    def whole(kk):
        return lead.at[:, 0:1] if kk == 0 else lead.at[:, 1:3]

    for kk in range(2):

        @pl.when(k == kk)
        def _():
            for i in range(1, NZ):
                zz = (z + i) % NZ
                wait_bytes(gathered(kk, zz), l3_recv.at[zz])
            remote(whole(kk), whole(kk), sib_send, sib_recv, sib, c).start()

    for kk in range(2):

        @pl.when(k != kk)
        def _():
            wait_bytes(whole(kk), sib_recv)

    def block(b):
        return lead[:, b].reshape(TILE, TILE)

    FIRST = (
        (1, lambda: own_column(2)),
        (2, lambda: other_columns(1)),
        (4, lambda: own_column(3)),
        (6, lambda: other_columns(2)),
    )
    SECOND = ((0, lambda: own_column(4)), (2, lambda: other_columns(3)))
    init_work(work, block(0))

    def first(g, _):
        eliminate(g, work)
        for at, service in FIRST:

            @pl.when(g == at)
            def _():
                service()

        return 0

    lax.fori_loop(0, TILE // NB, first, 0)
    inv_one = triangle(work[:, TILE:], True)
    inv[0:TILE, 0:TILE] = inv_one
    inv[0:TILE, TILE:PANEL] = jnp.zeros((TILE, TILE), F32)
    below = mul6(block(1), inv_one, NT)
    init_work(work, block(2) - mul6(below, below, NT))
    joint = mul6(below, inv_one, NN)

    for kk in range(2):

        @pl.when(k == kk)
        def _():
            wait_bytes(cols.at[kk], c_recv.at[0])
            wait_bytes(heads.at[kk], h_recv.at[0])
            remote(cols.at[kk], cols.at[kk], c_send.at[0], c_recv.at[1], sib, c).start()
            remote(heads.at[kk], heads.at[kk], h_send.at[0], h_recv.at[1], sib, c).start()

    def second(g, _):
        eliminate(g, work)
        for at, service in SECOND:

            @pl.when(g == at)
            def _():
                service()

        return 0

    lax.fori_loop(0, TILE // NB, second, 0)
    inv_two = triangle(work[:, TILE:], True)
    inv[TILE:PANEL, TILE:PANEL] = inv_two
    inv[TILE:PANEL, 0:TILE] = -mul6(inv_two, joint, NN)

    for kk in range(2):

        @pl.when(k != kk)
        def _():
            wait_bytes(cols.at[kk], c_recv.at[1])
            wait_bytes(heads.at[kk], h_recv.at[1])

    first_obs = jnp.concatenate([heads[0, 0:1, :], heads[1, 0:1, :]], 1)
    z_row = mul6(jnp.broadcast_to(first_obs, (8, PANEL)), inv[...], NT)[0:1, :]
    col_high[...], col_low[...] = split2(mul6(inv[...], cols[...].reshape(PANEL, 512), NN))
    i_h, i_m, i_l = split3(inv[...].T)
    lane = lax.broadcasted_iota(jnp.int32, (CHUNK, TILE), 1)
    r_at = lax.broadcasted_iota(jnp.int32, (CHUNK, PANEL), 0)
    c_at = lax.broadcasted_iota(jnp.int32, (CHUNK, PANEL), 1)

    def factor_block(n, _):
        off = jnp.where(n % 2 == 1, (n + 1) // 2, (NZ - n // 2) % NZ)
        zz = (z + off) % NZ
        s, h = zz // 2, zz % 2

        @pl.when(n == NZ - 1)
        def _():
            other_columns(NZ // 2)

        @pl.when(n > 0)
        def _():
            for i in range(1, NX):
                xx = (x + i) % NX
                wait_bytes(chunk(xx, zz, HALF, HALF), side_recv.at[zz, xx])

        p_h, p_m, p_l = split3(pan[s, :, h].reshape(PANEL, PANEL))
        small = mul(p_h, i_l, NN) + mul(p_l, i_h, NN) + mul(p_m, i_m, NN)
        part = small + (mul(p_h, i_m, NN) + mul(p_m, i_h, NN)) + mul(p_h, i_h, NN)
        rows[s, :, h] = part.reshape(NX, CHUNK, PANEL)

        @pl.when((r < 2) & (zz < 2))
        def _():
            rows[0, 0, h] = jnp.where(c_at <= r_at + CHUNK * h + TILE * r, rows[0, 0, h], 0.0)

        pltpu.make_async_copy(rows.at[s, :, h], fac_here.at[s, :, h], out_sem.at[n]).start()
        here = pl.ds(pl.multiple_of(CHUNK * h, CHUNK), CHUNK)
        sums = acc[here, :]
        for xx in range(NX):
            dots = jnp.sum(part[xx * CHUNK : (xx + 1) * CHUNK] * z_row, axis=1, keepdims=True)
            sums = jnp.where(lane == NX * s + xx, dots, sums)
        acc[here, :] = sums
        return 0

    acc[...] = jnp.zeros((TILE, TILE), F32)
    lax.fori_loop(0, NZ, factor_block, 0)
    load_obs.wait()
    white[...] = obs_here[...] - acc[...].T[0:16]

    @pl.when(r == 0)
    def _():
        white[0:1, :] = z_row[:, 0:TILE]

    @pl.when(r == 1)
    def _():
        white[0:1, :] = z_row[:, TILE:PANEL]

    load_cov.wait()
    for n in range(NZ):
        wait_bytes(rows.at[0, :, 0], out_sem.at[n])

    for i in range(NX):
        rows = CHUNK if i == 0 else HALF
        for d in range(1, NZ // 2 + 1):
            part = chunk(x, z, 0, rows if d < NZ // 2 else rows // 2)
            wait_bytes(part, up_send.at[i, d])
            wait_bytes(part, down_send.at[i, d])
    for j in range(1, NX):
        wait_bytes(own, x_send.at[j])
        for d in range(1, NZ):
            wait_bytes(chunk(x, z, HALF, HALF), side_send.at[d, j])
    for kk in range(2):

        @pl.when(k == kk)
        def _():
            for i in range(1, NZ):
                wait_bytes(mine(kk), l3_send.at[i])
            wait_bytes(whole(kk), sib_send)
            wait_bytes(cols.at[kk], c_send.at[0])
            wait_bytes(heads.at[kk], h_send.at[0])

        @pl.when(r == kk)
        def _():
            for i in range(1, 4):
                wait_bytes(cols.at[kk], c_send.at[i])
                wait_bytes(heads.at[kk], h_send.at[i])
            for i in range(1, NZ):
                wait_bytes(turn.at[0, 0:CHUNK, :], sc_send.at[i])

            @pl.when(z != kk)
            def _():
                wait_bytes(turn.at[0, 0:CHUNK, :], sc_send.at[0])

        @pl.when((r == kk) & in_root_plane)
        def _():
            for i in range(1, 16):
                wait_bytes(mine(kk), l2_send.at[i])

    @pl.when(((r < 2) & (c == 0)) | ((r == 1) & (c == 1)))
    def _():
        for i in range(NZ):

            @pl.when(z != i)
            def _():
                wait_bytes(lead.at[0, 0], l1_send.at[i])


def update_kernel(cov, rows, col_high, col_low, white_in, out, fac, white, done, sems):
    write_rows = pltpu.make_async_copy(rows, fac, sems.at[0])
    write_rows.start()
    c_h, c_l = col_high[...], col_low[...]
    writes = []
    for i in range(PARTS):
        n = 2048 // PARTS
        at = slice(i * n, (i + 1) * n)
        f_h, f_l = split2(rows[at, :])
        done[at, :] = cov[at, :] - (mul(f_h, c_l, NN) + mul(f_l, c_h, NN) + mul(f_h, c_h, NN))
        copy = pltpu.make_async_copy(done.at[at, :], out.at[at, :], sems.at[1 + i])
        copy.start()
        writes.append(copy)
    white[...] = white_in[...]
    write_rows.wait()
    for copy in writes:
        copy.wait()


def per_device(covariance, observations):
    obs = observations.reshape(16, TILE)
    dma = pltpu.SemaphoreType.DMA
    any_space = pl.BlockSpec(memory_space=pl.ANY)
    vmem = pl.BlockSpec(memory_space=pltpu.VMEM)
    fac_here, cov_here, col_high, col_low, white = pl.pallas_call(
        gather_kernel,
        out_shape=[
            jax.ShapeDtypeStruct((4, NX, 2, CHUNK, PANEL), F32),
            jax.ShapeDtypeStruct((2048, 512), F32),
            jax.ShapeDtypeStruct((PANEL, 512), BF16),
            jax.ShapeDtypeStruct((PANEL, 512), BF16),
            jax.ShapeDtypeStruct((16, TILE), F32),
        ],
        in_specs=[any_space, any_space],
        out_specs=[any_space, any_space, vmem, vmem, vmem],
        scratch_shapes=[
            pltpu.VMEM((4, NX, 2, CHUNK, PANEL), F32),
            pltpu.VMEM((2, TILE, 512), F32),
            pltpu.VMEM((2, 8, TILE), F32),
            pltpu.VMEM((16, TILE), F32),
            pltpu.VMEM((4, NX, 2, CHUNK, PANEL), F32),
            pltpu.VMEM((PANEL, PANEL), F32),
            pltpu.VMEM((TILE, TILE), F32),
            pltpu.VMEM((NZ, 3, SLICE, TILE), F32),
            pltpu.VMEM((4, TILE, TILE), F32),
            pltpu.VMEM((TILE, PANEL), F32),
            pltpu.VMEM((TILE, 512), F32),
            dma((3,)), dma((NZ,)),
            dma((8,)), dma((3,)), dma((16,)), dma, dma((8,)), dma((8,)), dma, dma,
            dma((8,)), dma((2,)), dma((4,)), dma((4,)),
            dma((4, 5)), dma((4, 5)), dma((4, 5)), dma((4, 5)), dma((8, 4)), dma((8, 4)),
            dma((4,)), dma((2,)), dma((4,)), dma((2,)),
        ],
        compiler_params=pltpu.CompilerParams(collective_id=0, has_side_effects=True, vmem_limit_bytes=46 << 20),
    )(covariance, obs)
    out, fac, white = pl.pallas_call(
        update_kernel,
        out_shape=[
            jax.ShapeDtypeStruct((2048, 512), F32),
            jax.ShapeDtypeStruct((2048, PANEL), F32),
            jax.ShapeDtypeStruct((16, TILE), F32),
        ],
        in_specs=[vmem] * 5,
        out_specs=[any_space, any_space, vmem],
        scratch_shapes=[
            pltpu.VMEM((2048, 512), F32),
            dma((1 + PARTS,)),
        ],
        compiler_params=pltpu.CompilerParams(vmem_limit_bytes=36 << 20),
    )(cov_here, fac_here.reshape(2048, PANEL), col_high, col_low, white)
    return out, fac, white.reshape(2048)


def solution(mesh):
    placed = (P("row", "col"), P("row"))
    return jax.shard_map(
        per_device,
        mesh=mesh,
        in_specs=placed,
        out_specs=(P("row", "col"), P("row", None), P("row")),
        check_vma=False,
    )
```

```python
import jax
import jax.numpy as jnp
from jax import lax
from jax.experimental import pallas as pl
from jax.experimental.pallas import tpu as pltpu
from jax.sharding import PartitionSpec as P

MESH = pl.DeviceIdType.MESH
TILE = 128
PANEL = 2 * TILE
NB = 16
N_ROW, N_COL, NX, NZ = 8, 32, 4, 8
CHUNK = 64
HALF = CHUNK // 2
QUARTER = CHUNK // 4
PARTS = 4
OWN = NX
SLICE = TILE // NZ
F32, BF16 = jnp.float32, jnp.bfloat16


def split3(x):
    high = x.astype(BF16)
    rest = x - high.astype(F32)
    mid = rest.astype(BF16)
    return high, mid, (rest - mid.astype(F32)).astype(BF16)


def split2(x):
    high = x.astype(BF16)
    return high, (x - high.astype(F32)).astype(BF16)


def mul(a, b, dims):
    return lax.dot_general(a, b, (dims, ((), ())), preferred_element_type=F32)


def mul6(a, b, dims):
    ah, am, al = split3(a)
    bh, bm, bl = split3(b)
    small = mul(ah, bl, dims) + mul(al, bh, dims) + mul(am, bm, dims)
    return small + (mul(ah, bm, dims) + mul(am, bh, dims)) + mul(ah, bh, dims)


NN, NT, TN = ((1,), (0,)), ((1,), (1,)), ((0,), (0,))


def triangle(x, keep_lower):
    r = lax.broadcasted_iota(jnp.int32, (TILE, TILE), 0)
    c = lax.broadcasted_iota(jnp.int32, (TILE, TILE), 1)
    return jnp.where(r >= c if keep_lower else r <= c, x, 0.0)


def init_work(work, block):
    r = lax.broadcasted_iota(jnp.int32, (TILE, TILE), 0)
    c = lax.broadcasted_iota(jnp.int32, (TILE, TILE), 1)
    work[:, :TILE] = block
    work[:, TILE:] = jnp.where(r == c, 1.0, 0.0).astype(F32)


def eliminate(g, work):
    base = g * NB
    here = pl.ds(pl.multiple_of(base, NB), NB)
    rows = work[here, :]
    turned = pltpu.roll(rows[:, :TILE], lax.rem(TILE - base, TILE), 1)
    sub = lax.broadcasted_iota(jnp.int32, (8, TILE), 0)

    def column(top, j):
        return jnp.broadcast_to(turned[top : top + 8, j : j + 1], (8, TILE))

    def spread(x, i):
        return jnp.broadcast_to(x[i : i + 1, :], (8, TILE))

    def factor(diag, others, sides):
        el = [[spread(diag[j], i) for j in range(i + 1)] for i in range(8)]
        top = sides[0]
        for j in range(8):
            inv = lax.rsqrt(el[j][j])
            low = [None] * 8
            for i in range(j + 1, 8):
                low[i] = el[i][j] * inv
            for i in range(j + 1, 8):
                for k in range(j + 1, i + 1):
                    el[i][k] = el[i][k] - low[i] * low[k]
            for cols in [diag] + others:
                cols[j] = cols[j] * inv
                for k in range(j + 1, 8):
                    cols[k] = cols[k] - cols[j] * low[k]
            below = jnp.where(sub > j, diag[j], 0.0)
            for n in range(2):
                row = spread(top[n], j) * inv
                top[n] = jnp.where(sub == j, row, top[n] - below * row)
                for cols, side in zip(others, sides[1:]):
                    side[n] = side[n] - cols[j] * row

    a11 = [column(0, j) for j in range(8)]
    a21 = [column(8, j) for j in range(8)]
    a22 = [column(8, 8 + j) for j in range(8)]
    r1 = [rows[0:8, :TILE], rows[0:8, TILE:]]
    r2 = [rows[8:16, :TILE], rows[8:16, TILE:]]
    factor(a11, [a21], [r1, r2])
    for k in range(8):
        for j in range(8):
            a22[k] = a22[k] - a21[j] * spread(a21[j], k)
    factor(a22, [], [r2])
    u_left = jnp.concatenate([r1[0], r2[0]], 0)
    u_right = jnp.concatenate([r1[1], r2[1]], 0)
    lane = lax.broadcasted_iota(jnp.int32, (NB, TILE), 1)
    below = jnp.where(lane >= base + NB, u_left, 0.0)
    u = jnp.concatenate([u_left, u_right], 1)
    h, m, l = split3(u)
    hb, mb, lb = split3(below)
    lhs = jnp.concatenate([hb, hb, mb, mb, hb, lb], 0)
    rhs = jnp.concatenate([h, m, h, m, l, h], 0)
    work[...] = work[...] - mul(lhs, rhs, TN)
    work[here, :] = u


def gather_kernel(
    cov, obs, fac_here, cov_here, col_high, col_low, white,
    pan, cols, heads, obs_here, rows, inv, acc, lead, turn, work, saved,
    load_sem, out_sem, l1_send, l1_recv, l2_send, l2_recv, l3_send, l3_recv, sib_send, sib_recv,
    sc_send, sc_recv, x_send, x_recv, up_send, up_recv, down_send, down_recv, side_send, side_recv,
    c_send, c_recv, h_send, h_recv,
):
    r, c = lax.axis_index("row"), lax.axis_index("col")
    y, k = r // 2, r % 2
    x, z = c // NZ, c % NZ
    sib = r + 1 - 2 * k

    def dev(rr, cc):
        return {"row": rr, "col": cc}

    def x_peer(i):
        return ((x + i) % NX) * NZ + z

    def z_peer(i):
        return x * NZ + (z + i) % NZ

    def remote(src, dst, send, recv, rr, cc):
        return pltpu.make_async_remote_copy(
            src_ref=src, dst_ref=dst, send_sem=send, recv_sem=recv, device_id=dev(rr, cc), device_id_type=MESH
        )

    at_source = r < 2
    in_root_plane = c < NZ

    @pl.when(at_source)
    def _():
        pltpu.make_async_copy(cov.at[0:TILE, :], saved, load_sem.at[0]).start()

    barrier = pltpu.get_barrier_semaphore()

    def hello(rr, cc):
        pl.semaphore_signal(barrier, inc=1, device_id=dev(rr, cc), device_id_type=MESH)

    for i in range(1, NX):
        hello(r, x_peer(i))
    for i in range(1, NZ):
        hello(r, z_peer(i))
    for i in range(1, 4):
        hello((r + 2 * i) % N_ROW, c)
    hello(sib, c)
    hello(0, x * NZ + r)
    hello(1, x * NZ + r)
    hello(k, z)
    @pl.when(at_source)
    def _():
        pltpu.make_async_copy(cov.at[0:TILE, :], saved, load_sem.at[0]).wait()
        for s in range(4):
            turn[s] = saved[:, s * TILE : (s + 1) * TILE].T

    due = 14 + jnp.where(at_source, NZ, 0) + jnp.where(at_source & in_root_plane, 16, 0)
    pl.semaphore_wait(barrier, due)

    def level_one(block, owner):
        for i in range(NZ):
            rows = slice(SLICE * i, SLICE * (i + 1))

            @pl.when(z != i)
            def _():
                remote(
                    cov.at[rows, 0:TILE], lead.at[i, block], l1_send.at[i], l1_recv.at[block], r, i
                ).start()

            @pl.when(z == i)
            def _():
                pltpu.make_async_copy(cov.at[rows, 0:TILE], lead.at[i, block], l1_recv.at[block]).start()

    @pl.when((r == 0) & (c == 0))
    def _():
        level_one(0, 0)

    @pl.when((r == 1) & (c == 0))
    def _():
        level_one(1, 0)

    @pl.when((r == 1) & (c == 1))
    def _():
        level_one(2, 1)

    def wait_bytes(ref, sem):
        pltpu.make_async_copy(ref, ref, sem).wait()

    def mine(kk):
        return lead.at[z, 0:1] if kk == 0 else lead.at[z, 1:3]

    def chunk(xx, zz, first, count, half=None):
        if half is None:
            return pan.at[zz // 2, xx, zz % 2, first : first + count, :]
        return pan.at[zz // 2, xx, zz % 2, first : first + count, half * TILE : (half + 1) * TILE]

    @pl.when(at_source)
    def _():
        for kk in range(2):

            @pl.when(r == kk)
            def _():
                for part in range(2):
                    for i in (4, 3, 5, 2, 6, 1, 7, 0):
                        zz = (z + i) % NZ
                        low = pl.multiple_of(CHUNK * (zz % 2) + HALF * part, HALF)
                        src = turn.at[zz // 2, pl.ds(low, HALF), :]
                        dst = chunk(x, zz, HALF * part, HALF, kk)
                        if i:
                            remote(src, dst, sc_send.at[part, i], sc_recv.at[kk, part], z, x * NZ + zz).start()
                        else:

                            @pl.when(z == kk)
                            def _():
                                pltpu.make_async_copy(src, dst, sc_recv.at[kk, part]).start()

                            @pl.when(z != kk)
                            def _():
                                remote(src, dst, sc_send.at[part, i], sc_recv.at[kk, part], z, x * NZ + zz).start()

    for kk in range(2):

        @pl.when((r == kk) & in_root_plane)
        def _():
            if kk == 0:
                wait_bytes(lead.at[z, 0], l1_recv.at[0])
            else:
                wait_bytes(lead.at[z, 1], l1_recv.at[1])
                wait_bytes(lead.at[z, 2], l1_recv.at[2])
            for yy in (2, 1, 3, 0):
                for xx in (2, 1, 3, 0):
                    if (yy, xx) != (0, 0):
                        remote(
                            mine(kk), mine(kk), l2_send.at[yy * NX + xx], l2_recv, 2 * yy + kk, xx * NZ + z
                        ).start()

    is_root_line = at_source & in_root_plane
    for kk in range(2):

        @pl.when(k == kk)
        def _():
            @pl.when(jnp.logical_not(is_root_line))
            def _():
                wait_bytes(mine(kk), l2_recv)

            for i in (4, 3, 5, 2, 6, 1, 7):
                remote(mine(kk), mine(kk), l3_send.at[i], l3_recv.at[z], r, z_peer(i)).start()

    def stream(i):
        return ((x + i) % NX, 0) if i < OWN else (x, HALF)

    def piece(i, zz, d, way):
        xx, first = stream(i)
        if d < NZ // 2:
            return chunk(xx, zz, first, HALF)
        return chunk(xx, zz, first if way == 1 else first + QUARTER, QUARTER)

    def push(i, d, way):
        send, recv = (up_send, up_recv) if way == 1 else (down_send, down_recv)
        part = piece(i, (z - way * (d - 1) + NZ) % NZ, d, way)
        remote(part, part, send.at[i, d], recv.at[i, d], r, x * NZ + (z + way + NZ) % NZ).start()

    def hop(i, d):
        for way, recv in ((1, up_recv), (-1, down_recv)):
            wait_bytes(piece(i, (z - way * d + NZ) % NZ, d, way), recv.at[i, d])
            if d < NZ // 2:
                push(i, d + 1, way)

    def sideways(zz, slot):
        part = chunk(x, zz, HALF, HALF)
        for j in (2, 1, 3):
            remote(part, part, side_send.at[slot, j], side_recv.at[zz, x], r, x_peer(j)).start()

    def own_column(d):
        hop(OWN, d)
        sideways((z - d + NZ) % NZ, d)
        if d < NZ // 2:
            sideways((z + d) % NZ, NZ - d)

    def other_columns(d):
        for i in (1, 3, 2):
            hop(i, d)

    for kk in range(2):
        wait_bytes(chunk(x, z, 0, HALF, kk), sc_recv.at[kk, 0])
    for i in (2, 1, 3):
        part = chunk(x, z, 0, HALF)
        remote(part, part, x_send.at[i], x_recv.at[x], r, x_peer(i)).start()
    for way in (1, -1):
        push(0, 1, way)
    for kk in range(2):
        wait_bytes(chunk(x, z, HALF, HALF, kk), sc_recv.at[kk, 1])
    for way in (1, -1):
        push(OWN, 1, way)
    sideways(z, 0)

    for kk in range(2):

        @pl.when(r == kk)
        def _():
            pltpu.make_async_copy(cov.at[0:TILE, :], cols.at[kk], c_recv.at[0]).start()
            pltpu.make_async_copy(obs.at[0:8, :], heads.at[kk], h_recv.at[0]).start()
            for i in range(1, 4):
                rr = (r + 2 * i) % N_ROW
                remote(cov.at[0:TILE, :], cols.at[kk], c_send.at[i], c_recv.at[0], rr, c).start()
                remote(obs.at[0:8, :], heads.at[kk], h_send.at[i], h_recv.at[0], rr, c).start()

    load_cov = pltpu.make_async_copy(cov, cov_here, load_sem.at[1])
    load_cov.start()
    load_obs = pltpu.make_async_copy(obs, obs_here, load_sem.at[2])
    load_obs.start()

    def gathered(kk, zz):
        return lead.at[zz, 0:1] if kk == 0 else lead.at[zz, 1:3]

    def whole(kk):
        return lead.at[:, 0:1] if kk == 0 else lead.at[:, 1:3]

    for kk in range(2):

        @pl.when(k == kk)
        def _():
            for i in range(1, NZ):
                zz = (z + i) % NZ
                wait_bytes(gathered(kk, zz), l3_recv.at[zz])
            remote(whole(kk), whole(kk), sib_send, sib_recv, sib, c).start()

    own_column(1)
    hop(0, 1)
    for i in (1, 3, 2):
        wait_bytes(chunk((x + i) % NX, z, 0, HALF), x_recv.at[(x + i) % NX])
        for way in (1, -1):
            push(i, 1, way)

    for kk in range(2):

        @pl.when(k != kk)
        def _():
            wait_bytes(whole(kk), sib_recv)

    def block(b):
        return lead[:, b].reshape(TILE, TILE)

    FIRST = ((3, lambda: own_column(2)), (4, lambda: hop(0, 2)), (6, lambda: other_columns(1)), )
    SECOND = ((0, lambda: own_column(3)), (1, lambda: hop(0, 3)), (2, lambda: other_columns(2)), (5, lambda: own_column(4)), (7, lambda: other_columns(3)), )
    init_work(work, block(0))

    def first(g, _):
        eliminate(g, work)
        for at, service in FIRST:

            @pl.when(g == at)
            def _():
                service()

        return 0

    lax.fori_loop(0, TILE // NB, first, 0)
    inv_one = triangle(work[:, TILE:], True)
    inv[0:TILE, 0:TILE] = inv_one
    inv[0:TILE, TILE:PANEL] = jnp.zeros((TILE, TILE), F32)
    below = mul6(block(1), inv_one, NT)
    init_work(work, block(2) - mul6(below, below, NT))
    joint = mul6(below, inv_one, NN)

    for kk in range(2):

        @pl.when(k == kk)
        def _():
            wait_bytes(cols.at[kk], c_recv.at[0])
            wait_bytes(heads.at[kk], h_recv.at[0])
            remote(cols.at[kk], cols.at[kk], c_send.at[0], c_recv.at[1], sib, c).start()
            remote(heads.at[kk], heads.at[kk], h_send.at[0], h_recv.at[1], sib, c).start()

    def second(g, _):
        eliminate(g, work)
        for at, service in SECOND:

            @pl.when(g == at)
            def _():
                service()

        return 0

    lax.fori_loop(0, TILE // NB, second, 0)
    inv_two = triangle(work[:, TILE:], True)
    inv[TILE:PANEL, TILE:PANEL] = inv_two
    inv[TILE:PANEL, 0:TILE] = -mul6(inv_two, joint, NN)

    for kk in range(2):

        @pl.when(k != kk)
        def _():
            wait_bytes(cols.at[kk], c_recv.at[1])
            wait_bytes(heads.at[kk], h_recv.at[1])

    first_obs = jnp.concatenate([heads[0, 0:1, :], heads[1, 0:1, :]], 1)
    z_row = mul6(jnp.broadcast_to(first_obs, (8, PANEL)), inv[...], NT)[0:1, :]
    col_high[...], col_low[...] = split2(mul6(inv[...], cols[...].reshape(PANEL, 512), NN))
    i_h, i_m, i_l = split3(inv[...].T)
    lane = lax.broadcasted_iota(jnp.int32, (CHUNK, TILE), 1)
    r_at = lax.broadcasted_iota(jnp.int32, (CHUNK, PANEL), 0)
    c_at = lax.broadcasted_iota(jnp.int32, (CHUNK, PANEL), 1)

    def factor_block(n, _):
        off = jnp.where(n % 2 == 1, (n + 1) // 2, (NZ - n // 2) % NZ)
        zz = (z + off) % NZ
        s, h = zz // 2, zz % 2

        @pl.when(n == NZ - 1)
        def _():
            hop(0, NZ // 2)
            other_columns(NZ // 2)

        for i in range(1, NX):
            xx = (x + i) % NX
            wait_bytes(chunk(xx, zz, HALF, HALF), side_recv.at[zz, xx])

        p_h, p_m, p_l = split3(pan[s, :, h].reshape(PANEL, PANEL))
        small = mul(p_h, i_l, NN) + mul(p_l, i_h, NN) + mul(p_m, i_m, NN)
        part = small + (mul(p_h, i_m, NN) + mul(p_m, i_h, NN)) + mul(p_h, i_h, NN)
        rows[s, :, h] = part.reshape(NX, CHUNK, PANEL)

        @pl.when((r < 2) & (zz < 2))
        def _():
            rows[0, 0, h] = jnp.where(c_at <= r_at + CHUNK * h + TILE * r, rows[0, 0, h], 0.0)

        pltpu.make_async_copy(rows.at[s, :, h], fac_here.at[s, :, h], out_sem.at[n]).start()
        here = pl.ds(pl.multiple_of(CHUNK * h, CHUNK), CHUNK)
        sums = acc[here, :]
        for xx in range(NX):
            dots = jnp.sum(part[xx * CHUNK : (xx + 1) * CHUNK] * z_row, axis=1, keepdims=True)
            sums = jnp.where(lane == NX * s + xx, dots, sums)
        acc[here, :] = sums
        return 0

    acc[...] = jnp.zeros((TILE, TILE), F32)
    lax.fori_loop(0, NZ, factor_block, 0)
    load_obs.wait()
    white[...] = obs_here[...] - acc[...].T[0:16]

    @pl.when(r == 0)
    def _():
        white[0:1, :] = z_row[:, 0:TILE]

    @pl.when(r == 1)
    def _():
        white[0:1, :] = z_row[:, TILE:PANEL]

    load_cov.wait()
    for n in range(NZ):
        wait_bytes(rows.at[0, :, 0], out_sem.at[n])

    for i in range(OWN + 1):
        for d in range(1, NZ // 2 + 1):
            wait_bytes(piece(i, z, d, 1), up_send.at[i, d])
            wait_bytes(piece(i, z, d, -1), down_send.at[i, d])
    for j in range(1, NX):
        wait_bytes(chunk(x, z, 0, HALF), x_send.at[j])
        for slot in range(NZ):
            wait_bytes(chunk(x, z, HALF, HALF), side_send.at[slot, j])
    for kk in range(2):

        @pl.when(k == kk)
        def _():
            for i in range(1, NZ):
                wait_bytes(mine(kk), l3_send.at[i])
            wait_bytes(whole(kk), sib_send)
            wait_bytes(cols.at[kk], c_send.at[0])
            wait_bytes(heads.at[kk], h_send.at[0])

        @pl.when(r == kk)
        def _():
            for i in range(1, 4):
                wait_bytes(cols.at[kk], c_send.at[i])
                wait_bytes(heads.at[kk], h_send.at[i])
            for part in range(2):
                for i in range(1, NZ):
                    wait_bytes(turn.at[0, 0:HALF, :], sc_send.at[part, i])

                @pl.when(z != kk)
                def _():
                    wait_bytes(turn.at[0, 0:HALF, :], sc_send.at[part, 0])

        @pl.when((r == kk) & in_root_plane)
        def _():
            for i in range(1, 16):
                wait_bytes(mine(kk), l2_send.at[i])

    @pl.when(((r < 2) & (c == 0)) | ((r == 1) & (c == 1)))
    def _():
        for i in range(NZ):

            @pl.when(z != i)
            def _():
                wait_bytes(lead.at[0, 0], l1_send.at[i])


def update_kernel(cov, rows, col_high, col_low, white_in, out, fac, white, done, sems):
    write_rows = pltpu.make_async_copy(rows, fac, sems.at[0])
    write_rows.start()
    c_h, c_l = col_high[...], col_low[...]
    writes = []
    for i in range(PARTS):
        n = 2048 // PARTS
        at = slice(i * n, (i + 1) * n)
        f_h, f_l = split2(rows[at, :])
        done[at, :] = cov[at, :] - (mul(f_h, c_l, NN) + mul(f_l, c_h, NN) + mul(f_h, c_h, NN))
        copy = pltpu.make_async_copy(done.at[at, :], out.at[at, :], sems.at[1 + i])
        copy.start()
        writes.append(copy)
    white[...] = white_in[...]
    write_rows.wait()
    for copy in writes:
        copy.wait()


def per_device(covariance, observations):
    obs = observations.reshape(16, TILE)
    dma = pltpu.SemaphoreType.DMA
    any_space = pl.BlockSpec(memory_space=pl.ANY)
    vmem = pl.BlockSpec(memory_space=pltpu.VMEM)
    fac_here, cov_here, col_high, col_low, white = pl.pallas_call(
        gather_kernel,
        out_shape=[
            jax.ShapeDtypeStruct((4, NX, 2, CHUNK, PANEL), F32),
            jax.ShapeDtypeStruct((2048, 512), F32),
            jax.ShapeDtypeStruct((PANEL, 512), BF16),
            jax.ShapeDtypeStruct((PANEL, 512), BF16),
            jax.ShapeDtypeStruct((16, TILE), F32),
        ],
        in_specs=[any_space, any_space],
        out_specs=[any_space, any_space, vmem, vmem, vmem],
        scratch_shapes=[
            pltpu.VMEM((4, NX, 2, CHUNK, PANEL), F32),
            pltpu.VMEM((2, TILE, 512), F32),
            pltpu.VMEM((2, 8, TILE), F32),
            pltpu.VMEM((16, TILE), F32),
            pltpu.VMEM((4, NX, 2, CHUNK, PANEL), F32),
            pltpu.VMEM((PANEL, PANEL), F32),
            pltpu.VMEM((TILE, TILE), F32),
            pltpu.VMEM((NZ, 3, SLICE, TILE), F32),
            pltpu.VMEM((4, TILE, TILE), F32),
            pltpu.VMEM((TILE, PANEL), F32),
            pltpu.VMEM((TILE, 512), F32),
            dma((3,)), dma((NZ,)),
            dma((8,)), dma((3,)), dma((16,)), dma, dma((8,)), dma((8,)), dma, dma,
            dma((2, 8)), dma((2, 2)), dma((4,)), dma((4,)),
            dma((5, 5)), dma((5, 5)), dma((5, 5)), dma((5, 5)), dma((8, 4)), dma((8, 4)),
            dma((4,)), dma((2,)), dma((4,)), dma((2,)),
        ],
        compiler_params=pltpu.CompilerParams(collective_id=0, has_side_effects=True, vmem_limit_bytes=46 << 20),
    )(covariance, obs)
    out, fac, white = pl.pallas_call(
        update_kernel,
        out_shape=[
            jax.ShapeDtypeStruct((2048, 512), F32),
            jax.ShapeDtypeStruct((2048, PANEL), F32),
            jax.ShapeDtypeStruct((16, TILE), F32),
        ],
        in_specs=[vmem] * 5,
        out_specs=[any_space, any_space, vmem],
        scratch_shapes=[
            pltpu.VMEM((2048, 512), F32),
            dma((1 + PARTS,)),
        ],
        compiler_params=pltpu.CompilerParams(vmem_limit_bytes=36 << 20),
    )(cov_here, fac_here.reshape(2048, PANEL), col_high, col_low, white)
    return out, fac, white.reshape(2048)


def solution(mesh):
    placed = (P("row", "col"), P("row"))
    return jax.shard_map(
        per_device,
        mesh=mesh,
        in_specs=placed,
        out_specs=(P("row", "col"), P("row", None), P("row")),
        check_vma=False,
    )
```

```python
import jax
import jax.numpy as jnp
from jax import lax
from jax.experimental import pallas as pl
from jax.experimental.pallas import tpu as pltpu
from jax.sharding import PartitionSpec as P

MESH = pl.DeviceIdType.MESH
TILE = 128
PANEL = 2 * TILE
NB = 16
N_ROW, N_COL, NX, NZ = 8, 32, 4, 8
CHUNK = 64
HALF = CHUNK // 2
QUARTER = CHUNK // 4
PARTS = 4
OWN = NX
SLICE = TILE // NZ
F32, BF16 = jnp.float32, jnp.bfloat16


def split3(x):
    high = x.astype(BF16)
    rest = x - high.astype(F32)
    mid = rest.astype(BF16)
    return high, mid, (rest - mid.astype(F32)).astype(BF16)


def split2(x):
    high = x.astype(BF16)
    return high, (x - high.astype(F32)).astype(BF16)


def mul(a, b, dims):
    return lax.dot_general(a, b, (dims, ((), ())), preferred_element_type=F32)


def mul6(a, b, dims):
    ah, am, al = split3(a)
    bh, bm, bl = split3(b)
    small = mul(ah, bl, dims) + mul(al, bh, dims) + mul(am, bm, dims)
    return small + (mul(ah, bm, dims) + mul(am, bh, dims)) + mul(ah, bh, dims)


NN, NT, TN = ((1,), (0,)), ((1,), (1,)), ((0,), (0,))


def triangle(x, keep_lower):
    r = lax.broadcasted_iota(jnp.int32, (TILE, TILE), 0)
    c = lax.broadcasted_iota(jnp.int32, (TILE, TILE), 1)
    return jnp.where(r >= c if keep_lower else r <= c, x, 0.0)


def init_work(work, block):
    r = lax.broadcasted_iota(jnp.int32, (TILE, TILE), 0)
    c = lax.broadcasted_iota(jnp.int32, (TILE, TILE), 1)
    work[:, :TILE] = block
    work[:, TILE:] = jnp.where(r == c, 1.0, 0.0).astype(F32)


def eliminate(g, work):
    base = g * NB
    here = pl.ds(pl.multiple_of(base, NB), NB)
    rows = work[here, :]
    turned = pltpu.roll(rows[:, :TILE], lax.rem(TILE - base, TILE), 1)
    sub = lax.broadcasted_iota(jnp.int32, (8, TILE), 0)

    def column(top, j):
        return jnp.broadcast_to(turned[top : top + 8, j : j + 1], (8, TILE))

    def spread(x, i):
        return jnp.broadcast_to(x[i : i + 1, :], (8, TILE))

    def factor(diag, others, sides):
        el = [[spread(diag[j], i) for j in range(i + 1)] for i in range(8)]
        top = sides[0]
        for j in range(8):
            inv = lax.rsqrt(el[j][j])
            low = [None] * 8
            for i in range(j + 1, 8):
                low[i] = el[i][j] * inv
            for i in range(j + 1, 8):
                for k in range(j + 1, i + 1):
                    el[i][k] = el[i][k] - low[i] * low[k]
            for cols in [diag] + others:
                cols[j] = cols[j] * inv
                for k in range(j + 1, 8):
                    cols[k] = cols[k] - cols[j] * low[k]
            below = jnp.where(sub > j, diag[j], 0.0)
            for n in range(2):
                row = spread(top[n], j) * inv
                top[n] = jnp.where(sub == j, row, top[n] - below * row)
                for cols, side in zip(others, sides[1:]):
                    side[n] = side[n] - cols[j] * row

    a11 = [column(0, j) for j in range(8)]
    a21 = [column(8, j) for j in range(8)]
    a22 = [column(8, 8 + j) for j in range(8)]
    r1 = [rows[0:8, :TILE], rows[0:8, TILE:]]
    r2 = [rows[8:16, :TILE], rows[8:16, TILE:]]
    factor(a11, [a21], [r1, r2])
    for k in range(8):
        for j in range(8):
            a22[k] = a22[k] - a21[j] * spread(a21[j], k)
    factor(a22, [], [r2])
    u_left = jnp.concatenate([r1[0], r2[0]], 0)
    u_right = jnp.concatenate([r1[1], r2[1]], 0)
    lane = lax.broadcasted_iota(jnp.int32, (NB, TILE), 1)
    below = jnp.where(lane >= base + NB, u_left, 0.0)
    u = jnp.concatenate([u_left, u_right], 1)
    h, m, l = split3(u)
    hb, mb, lb = split3(below)
    lhs = jnp.concatenate([hb, hb, mb, mb, hb, lb], 0)
    rhs = jnp.concatenate([h, m, h, m, l, h], 0)
    work[...] = work[...] - mul(lhs, rhs, TN)
    work[here, :] = u


def gather_kernel(
    cov, obs, rows, cov_here, col_high, col_low, white,
    pan, cols, heads, obs_here, inv, acc, lead, turn, work, saved,
    load_sem, l1_send, l1_recv, l2_send, l2_recv, l3_send, l3_recv, sib_send, sib_recv,
    sc_send, sc_recv, ring_send, x_recv, up_recv, down_recv, side_recv,
    c_send, c_recv, h_send, h_recv,
):
    r, c = lax.axis_index("row"), lax.axis_index("col")
    y, k = r // 2, r % 2
    x, z = c // NZ, c % NZ
    sib = r + 1 - 2 * k

    def dev(rr, cc):
        return {"row": rr, "col": cc}

    def x_peer(i):
        return ((x + i) % NX) * NZ + z

    def z_peer(i):
        return x * NZ + (z + i) % NZ

    def remote(src, dst, send, recv, rr, cc):
        return pltpu.make_async_remote_copy(
            src_ref=src, dst_ref=dst, send_sem=send, recv_sem=recv, device_id=dev(rr, cc), device_id_type=MESH
        )

    at_source = r < 2
    in_root_plane = c < NZ

    @pl.when(at_source)
    def _():
        pltpu.make_async_copy(cov.at[0:TILE, :], saved, load_sem.at[0]).start()

    barrier = pltpu.get_barrier_semaphore()

    def hello(rr, cc):
        pl.semaphore_signal(barrier, inc=1, device_id=dev(rr, cc), device_id_type=MESH)

    hello(0, x * NZ + r)
    hello(1, x * NZ + r)
    hello(k, z)
    for i in (4, 3, 5, 2, 6, 1, 7):
        hello(r, z_peer(i))
    for i in (2, 1, 3):
        hello(r, x_peer(i))
    for i in (2, 1, 3):
        hello((r + 2 * i) % N_ROW, c)
    hello(sib, c)

    @pl.when(at_source)
    def _():
        pltpu.make_async_copy(cov.at[0:TILE, :], saved, load_sem.at[0]).wait()
        for s in range(4):
            turn[s] = saved[:, s * TILE : (s + 1) * TILE].T

    due = 14 + jnp.where(at_source, NZ, 0) + jnp.where(at_source & in_root_plane, 16, 0)
    pl.semaphore_wait(barrier, due)

    def level_one(block, owner):
        for i in range(NZ):
            rows = slice(SLICE * i, SLICE * (i + 1))

            @pl.when(z != i)
            def _():
                remote(
                    cov.at[rows, 0:TILE], lead.at[i, block], l1_send, l1_recv.at[block], r, i
                ).start()

            @pl.when(z == i)
            def _():
                pltpu.make_async_copy(cov.at[rows, 0:TILE], lead.at[i, block], l1_recv.at[block]).start()

    @pl.when((r == 0) & (c == 0))
    def _():
        level_one(0, 0)

    @pl.when((r == 1) & (c == 0))
    def _():
        level_one(1, 0)

    @pl.when((r == 1) & (c == 1))
    def _():
        level_one(2, 1)

    def kib(n):
        if n % 16 == 0:
            return cov_here.at[0 : n // 2, :]
        return work.at[0:n, :] if n % 8 == 0 else cols.at[0, 0:8, 0 : n * 32]

    def wait_bytes(ref, sem):
        pltpu.make_async_copy(ref, ref, sem).wait()

    def mine(kk):
        return lead.at[z, 0:1] if kk == 0 else lead.at[z, 1:3]

    def chunk(xx, zz, first, count, half=None):
        if half is None:
            return pan.at[zz // 2, xx, zz % 2, first : first + count, :]
        return pan.at[zz // 2, xx, zz % 2, first : first + count, half * TILE : (half + 1) * TILE]

    @pl.when(at_source)
    def _():
        for kk in range(2):

            @pl.when(r == kk)
            def _():
                for part in range(2):
                    for i in (4, 3, 5, 2, 6, 1, 7, 0):
                        zz = (z + i) % NZ
                        low = pl.multiple_of(CHUNK * (zz % 2) + HALF * part, HALF)
                        src = turn.at[zz // 2, pl.ds(low, HALF), :]
                        dst = chunk(x, zz, HALF * part, HALF, kk)
                        if i:
                            remote(src, dst, sc_send, sc_recv.at[kk, part], z, x * NZ + zz).start()
                        else:

                            @pl.when(z == kk)
                            def _():
                                pltpu.make_async_copy(src, dst, sc_recv.at[kk, part]).start()

                            @pl.when(z != kk)
                            def _():
                                remote(src, dst, sc_send, sc_recv.at[kk, part], z, x * NZ + zz).start()

    for kk in range(2):

        @pl.when((r == kk) & in_root_plane)
        def _():
            if kk == 0:
                wait_bytes(lead.at[z, 0], l1_recv.at[0])
            else:
                wait_bytes(lead.at[z, 1], l1_recv.at[1])
                wait_bytes(lead.at[z, 2], l1_recv.at[2])
            for yy in (2, 1, 3, 0):
                for xx in (2, 1, 3, 0):
                    if (yy, xx) != (0, 0):
                        remote(
                            mine(kk), mine(kk), l2_send, l2_recv, 2 * yy + kk, xx * NZ + z
                        ).start()

    def stream(i):
        return ((x + i) % NX, 0) if i < OWN else (x, HALF)

    def piece(i, zz, d, way):
        xx, first = stream(i)
        if d < NZ // 2:
            return chunk(xx, zz, first, HALF)
        return chunk(xx, zz, first if way == 1 else first + QUARTER, QUARTER)

    def push(i, d, way):
        recv = up_recv if way == 1 else down_recv
        part = piece(i, (z - way * (d - 1) + NZ) % NZ, d, way)
        remote(part, part, ring_send, recv.at[i, d], r, x * NZ + (z + way + NZ) % NZ).start()

    def hop(i, d):
        for way, recv in ((1, up_recv), (-1, down_recv)):
            wait_bytes(piece(i, (z - way * d + NZ) % NZ, d, way), recv.at[i, d])
            if d < NZ // 2:
                push(i, d + 1, way)

    def sideways(zz):
        part = chunk(x, zz, HALF, HALF)
        for j in (2, 1, 3):
            remote(part, part, ring_send, side_recv.at[zz], r, x_peer(j)).start()

    def own_column(d):
        hop(OWN, d)
        sideways((z - d + NZ) % NZ)
        if d < NZ // 2:
            sideways((z + d) % NZ)

    def other_columns(d):
        for i in (1, 3, 2):
            hop(i, d)

    for kk in range(2):
        wait_bytes(chunk(x, z, 0, HALF, kk), sc_recv.at[kk, 0])
    for i in (2, 1, 3):
        part = chunk(x, z, 0, HALF)
        remote(part, part, ring_send, x_recv.at[x], r, x_peer(i)).start()
    for way in (1, -1):
        push(0, 1, way)
    is_root_line = at_source & in_root_plane
    for kk in range(2):

        @pl.when(k == kk)
        def _():
            @pl.when(jnp.logical_not(is_root_line))
            def _():
                wait_bytes(mine(kk), l2_recv)

            for i in (4, 3, 5, 2, 6, 1, 7):
                remote(mine(kk), mine(kk), l3_send, l3_recv.at[z], r, z_peer(i)).start()

    for kk in range(2):
        wait_bytes(chunk(x, z, HALF, HALF, kk), sc_recv.at[kk, 1])
    for way in (1, -1):
        push(OWN, 1, way)
    sideways(z)

    for kk in range(2):

        @pl.when(r == kk)
        def _():
            pltpu.make_async_copy(cov.at[0:TILE, :], cols.at[kk], c_recv.at[0]).start()
            pltpu.make_async_copy(obs.at[0:8, :], heads.at[kk], h_recv.at[0]).start()
            for i in range(1, 4):
                rr = (r + 2 * i) % N_ROW
                remote(cov.at[0:TILE, :], cols.at[kk], c_send.at[1], c_recv.at[0], rr, c).start()
                remote(obs.at[0:8, :], heads.at[kk], h_send.at[1], h_recv.at[0], rr, c).start()

    load_cov = pltpu.make_async_copy(cov, cov_here, load_sem.at[1])
    load_cov.start()
    load_obs = pltpu.make_async_copy(obs, obs_here, load_sem.at[2])
    load_obs.start()

    def gathered(kk, zz):
        return lead.at[zz, 0:1] if kk == 0 else lead.at[zz, 1:3]

    def whole(kk):
        return lead.at[:, 0:1] if kk == 0 else lead.at[:, 1:3]

    for kk in range(2):

        @pl.when(k == kk)
        def _():
            for i in range(1, NZ):
                zz = (z + i) % NZ
                wait_bytes(gathered(kk, zz), l3_recv.at[zz])
            remote(whole(kk), whole(kk), sib_send, sib_recv, sib, c).start()

    own_column(1)
    hop(0, 1)
    for i in (1, 3, 2):
        wait_bytes(chunk((x + i) % NX, z, 0, HALF), x_recv.at[(x + i) % NX])
        for way in (1, -1):
            push(i, 1, way)

    @pl.when(k == 1)
    def _():
        wait_bytes(whole(0), sib_recv)

    def block(b):
        return lead[:, b].reshape(TILE, TILE)

    FIRST = ((3, lambda: own_column(2)), (3, lambda: hop(0, 2)), (5, lambda: hop(1, 1)), (6, lambda: hop(3, 1)), (6, lambda: hop(2, 1)), )
    SECOND = ((0, lambda: own_column(3)), (0, lambda: hop(0, 3)), (1, lambda: hop(1, 2)), (2, lambda: hop(3, 2)), (2, lambda: hop(2, 2)), (5, lambda: own_column(4)), (6, lambda: hop(1, 3)), (7, lambda: hop(3, 3)), (7, lambda: hop(2, 3)), )
    init_work(work, block(0))

    def first(g, _):
        eliminate(g, work)
        for at, service in FIRST:

            @pl.when(g == at)
            def _():
                service()

        return 0

    lax.fori_loop(0, TILE // NB, first, 0)
    inv_one = triangle(work[:, TILE:], True)
    inv[0:TILE, 0:TILE] = inv_one
    inv[0:TILE, TILE:PANEL] = jnp.zeros((TILE, TILE), F32)

    @pl.when(k == 0)
    def _():
        wait_bytes(whole(1), sib_recv)

    below = mul6(block(1), inv_one, NT)
    init_work(work, block(2) - mul6(below, below, NT))
    joint = mul6(below, inv_one, NN)

    for kk in range(2):

        @pl.when(k == kk)
        def _():
            wait_bytes(cols.at[kk], c_recv.at[0])
            wait_bytes(heads.at[kk], h_recv.at[0])
            remote(cols.at[kk], cols.at[kk], c_send.at[0], c_recv.at[1], sib, c).start()
            remote(heads.at[kk], heads.at[kk], h_send.at[0], h_recv.at[1], sib, c).start()

    def second(g, _):
        eliminate(g, work)
        for at, service in SECOND:

            @pl.when(g == at)
            def _():
                service()

        return 0

    lax.fori_loop(0, TILE // NB, second, 0)
    inv_two = triangle(work[:, TILE:], True)
    inv[TILE:PANEL, TILE:PANEL] = inv_two
    inv[TILE:PANEL, 0:TILE] = -mul6(inv_two, joint, NN)

    for kk in range(2):

        @pl.when(k != kk)
        def _():
            wait_bytes(cols.at[kk], c_recv.at[1])
            wait_bytes(heads.at[kk], h_recv.at[1])

    first_obs = jnp.concatenate([heads[0, 0:1, :], heads[1, 0:1, :]], 1)
    z_row = mul6(jnp.broadcast_to(first_obs, (8, PANEL)), inv[...], NT)[0:1, :]
    i_h, i_m, i_l = split3(inv[...].T)
    lane = lax.broadcasted_iota(jnp.int32, (CHUNK, TILE), 1)
    r_at = lax.broadcasted_iota(jnp.int32, (CHUNK, PANEL), 0)
    c_at = lax.broadcasted_iota(jnp.int32, (CHUNK, PANEL), 1)

    def factor_block(n, _):
        off = jnp.where(n % 2 == 1, (n + 1) // 2, (NZ - n // 2) % NZ)
        zz = (z + off) % NZ
        s, h = zz // 2, zz % 2

        @pl.when(n == NZ - 2)
        def _():
            col_high[...], col_low[...] = split2(mul6(inv[...], cols[...].reshape(PANEL, 512), NN))

        @pl.when(n == NZ - 1)
        def _():
            hop(0, NZ // 2)
            other_columns(NZ // 2)

        wait_bytes(kib((NX - 1) * HALF), side_recv.at[zz])

        p_h, p_m, p_l = split3(pan[s, :, h].reshape(PANEL, PANEL))
        small = mul(p_h, i_l, NN) + mul(p_l, i_h, NN) + mul(p_m, i_m, NN)
        part = small + (mul(p_h, i_m, NN) + mul(p_m, i_h, NN)) + mul(p_h, i_h, NN)
        rows[s, :, h] = part.reshape(NX, CHUNK, PANEL)

        @pl.when((r < 2) & (zz < 2))
        def _():
            rows[0, 0, h] = jnp.where(c_at <= r_at + CHUNK * h + TILE * r, rows[0, 0, h], 0.0)

        here = pl.ds(pl.multiple_of(CHUNK * h, CHUNK), CHUNK)
        sums = acc[here, :]
        for xx in range(NX):
            dots = jnp.sum(part[xx * CHUNK : (xx + 1) * CHUNK] * z_row, axis=1, keepdims=True)
            sums = jnp.where(lane == NX * s + xx, dots, sums)
        acc[here, :] = sums
        return 0

    acc[...] = jnp.zeros((TILE, TILE), F32)
    lax.fori_loop(0, NZ, factor_block, 0)
    load_obs.wait()
    white[...] = obs_here[...] - acc[...].T[0:16]

    @pl.when(r == 0)
    def _():
        white[0:1, :] = z_row[:, 0:TILE]

    @pl.when(r == 1)
    def _():
        white[0:1, :] = z_row[:, TILE:PANEL]

    load_cov.wait()

    passed = 2 * (OWN + 1) * (NZ // 2 - 1) * HALF + 2 * (OWN + 1) * QUARTER
    wait_bytes(kib(passed + (NX - 1) * (NZ + 1) * HALF), ring_send)
    for kk in range(2):

        @pl.when(k == kk)
        def _():
            wait_bytes(kib((NZ - 1) * (kk + 1) * 8), l3_send)
            wait_bytes(whole(kk), sib_send)
            wait_bytes(cols.at[kk], c_send.at[0])
            wait_bytes(heads.at[kk], h_send.at[0])

        @pl.when(r == kk)
        def _():
            wait_bytes(kib(3 * 256), c_send.at[1])
            wait_bytes(kib(3 * 4), h_send.at[1])

            @pl.when(z != kk)
            def _():
                wait_bytes(kib(2 * NZ * 16), sc_send)

            @pl.when(z == kk)
            def _():
                wait_bytes(kib(2 * (NZ - 1) * 16), sc_send)

        @pl.when((r == kk) & in_root_plane)
        def _():
            wait_bytes(kib(15 * (kk + 1) * 8), l2_send)

    @pl.when(((r < 2) & (c == 0)) | ((r == 1) & (c == 1)))
    def _():
        wait_bytes(kib((NZ - 1) * 8), l1_send)


def update_kernel(cov, rows, col_high, col_low, white_in, out, fac, white, done, sems):
    write_rows = pltpu.make_async_copy(rows, fac, sems.at[0])
    write_rows.start()
    c_h, c_l = col_high[...], col_low[...]
    writes = []
    for i in range(PARTS):
        n = 2048 // PARTS
        at = slice(i * n, (i + 1) * n)
        f_h, f_l = split2(rows[at, :])
        done[at, :] = cov[at, :] - (mul(f_h, c_l, NN) + mul(f_l, c_h, NN) + mul(f_h, c_h, NN))
        copy = pltpu.make_async_copy(done.at[at, :], out.at[at, :], sems.at[1 + i])
        copy.start()
        writes.append(copy)
    white[...] = white_in[...]
    write_rows.wait()
    for copy in writes:
        copy.wait()


def per_device(covariance, observations):
    obs = observations.reshape(16, TILE)
    dma = pltpu.SemaphoreType.DMA
    any_space = pl.BlockSpec(memory_space=pl.ANY)
    vmem = pl.BlockSpec(memory_space=pltpu.VMEM)
    fac_here, cov_here, col_high, col_low, white = pl.pallas_call(
        gather_kernel,
        out_shape=[
            jax.ShapeDtypeStruct((4, NX, 2, CHUNK, PANEL), F32),
            jax.ShapeDtypeStruct((2048, 512), F32),
            jax.ShapeDtypeStruct((PANEL, 512), BF16),
            jax.ShapeDtypeStruct((PANEL, 512), BF16),
            jax.ShapeDtypeStruct((16, TILE), F32),
        ],
        in_specs=[any_space, any_space],
        out_specs=[vmem, any_space, vmem, vmem, vmem],
        scratch_shapes=[
            pltpu.VMEM((4, NX, 2, CHUNK, PANEL), F32),
            pltpu.VMEM((2, TILE, 512), F32),
            pltpu.VMEM((2, 8, TILE), F32),
            pltpu.VMEM((16, TILE), F32),
            pltpu.VMEM((PANEL, PANEL), F32),
            pltpu.VMEM((TILE, TILE), F32),
            pltpu.VMEM((NZ, 3, SLICE, TILE), F32),
            pltpu.VMEM((4, TILE, TILE), F32),
            pltpu.VMEM((TILE, PANEL), F32),
            pltpu.VMEM((TILE, 512), F32),
            dma((3,)),
            dma, dma((3,)), dma, dma, dma, dma((8,)), dma, dma,
            dma, dma((2, 2)), dma, dma((4,)), dma((5, 5)), dma((5, 5)), dma((8,)),
            dma((2,)), dma((2,)), dma((2,)), dma((2,)),
        ],
        compiler_params=pltpu.CompilerParams(collective_id=0, has_side_effects=True, vmem_limit_bytes=46 << 20),
    )(covariance, obs)
    out, fac, white = pl.pallas_call(
        update_kernel,
        out_shape=[
            jax.ShapeDtypeStruct((2048, 512), F32),
            jax.ShapeDtypeStruct((2048, PANEL), F32),
            jax.ShapeDtypeStruct((16, TILE), F32),
        ],
        in_specs=[vmem] * 5,
        out_specs=[any_space, any_space, vmem],
        scratch_shapes=[
            pltpu.VMEM((2048, 512), F32),
            dma((1 + PARTS,)),
        ],
        compiler_params=pltpu.CompilerParams(vmem_limit_bytes=36 << 20),
    )(cov_here, fac_here.reshape(2048, PANEL), col_high, col_low, white)
    return out, fac, white.reshape(2048)


def solution(mesh):
    placed = (P("row", "col"), P("row"))
    return jax.shard_map(
        per_device,
        mesh=mesh,
        in_specs=placed,
        out_specs=(P("row", "col"), P("row", None), P("row")),
        check_vma=False,
    )
```
